32 devices in a mesh: grp: 8 (over z, x), dp: 4 (over y, core).
Axes of the slice: x: 2, y: 2, z: 4, core: 2. Of those that a mesh axis runs over, the one named last changes fastest.
Arguments:
- queries: bfloat16 [4096, 4096], P(('grp', 'dp')), may hold values from -1.25 to 1.25
- documents: bfloat16 [4096, 4096], P(('grp', 'dp')), may hold values from -0.75 to 0.75
- positives: int32 [4096], P(('grp', 'dp')), may hold values from 0 to 127, as said below
- inner_owner: int32 [8, 512, 1], P('grp'), may hold values from 0 to 3; in each aligned block of 128 rows (0 to 127, 128 to 255, ..., all dimensions but the last counted through in order) at most 64 rows name the same one
- inner_row: int32 [8, 512, 1], P('grp'), may hold values from 0 to 127
- outer_owner: int32 [4, 8, 128, 1], P('dp'), may hold values from 0 to 6; in each aligned block of 128 rows (0 to 127, 128 to 255, ..., all dimensions but the last counted through in order) at most 36 rows name the same one
- outer_row: int32 [4, 8, 128, 1], P('dp'), may hold values from 0 to 127
Outputs:
- losses: float32 [4096], P(('grp', 'dp'))
- query_grads: bfloat16 [4096, 4096], P(('grp', 'dp'))
- doc_grads: bfloat16 [4096, 4096], P(('grp', 'dp'))
The draws below stay inside these ranges and needn't reach their ends.
Inputs may be any that keep to these rules, and one draw needn't show every extreme that they name: `positives`: within each device's 128 queries every row of that device's documents is the positive of exactly one query. `inner_owner`: among the 128 queries of one device, no dp index is named by more than 64 of them, a bound that some block reaches. `outer_owner`: among the 128 queries of one device, no value is named by more than 36 of them, a bound that some block reaches.
All inputs are finite; a program needn't handle non-finite values.
Results may differ from the reference program's by a relative error of at most 0.0041.
Values may be sent and summed in bfloat16 or wider, within the bound.
No kernel may reach another device: no remote copies, remote signals or barrier semaphores. Data moves between devices by JAX's collectives and lax.ppermute only.
A program may use at most 64 MiB of HBM per device.

```python
import math
import jax
import jax.numpy as jnp
import numpy as np
from jax import lax

D = 4096
Q_DEV = 128
CAP_IN = 64
CAP_OUT = 36
TOKENS = 4096
N_GRP = 8
N_DP = 4


def document_normals(key):
    folded = jax.random.fold_in(key, 7)
    return jax.random.truncated_normal(folded, -6.0, 6.0, (TOKENS, D), jnp.float32) * 0.125


def pair_rows(key):
    folded = jax.random.fold_in(key, 9)
    block_keys = jax.random.split(folded, TOKENS // Q_DEV)
    orders = jax.vmap(lambda single: jax.random.permutation(single, Q_DEV))(block_keys)
    return orders.reshape(TOKENS).astype(jnp.int32)


def draw_documents(key, part):
    normals = document_normals(key)
    values = normals
    return values.astype(jnp.bfloat16)


def draw_positives(key, part):
    return pair_rows(key)


def draw_queries(key, part):
    key = jax.random.fold_in(key, 23)
    query_key = jax.random.fold_in(key, 0)
    values = jax.random.truncated_normal(query_key, -6.0, 6.0, (TOKENS, D), jnp.float32) * 0.125
    return values.astype(jnp.bfloat16)


def touch_ends(values, stream_key, smallest, high):
    index_at = [jax.random.randint(jax.random.fold_in(stream_key, axis), (), 0, length) for axis, length in enumerate(values.shape)]
    longest = values.shape.index(max(values.shape))
    neighbour = index_at[:longest] + [(index_at[longest] + 1) % values.shape[longest]] + index_at[longest + 1:]
    return values.at[tuple(index_at)].set(smallest).at[tuple(neighbour)].set(high)


def deal_out(stream_key, own, number, rows, number_of, top, most, slope):
    ranking = jax.random.permutation(stream_key, number_of)
    heavy_load, common = portions_of(number_of, rows * top, most, slope, True), portions_of(number_of, rows * top, most, slope, False)
    places = jnp.arange(number_of)

    def named(tallies, turn):
        used = int((tallies > 0).sum())
        fixed = max(1, used // 4)
        shifted = fixed + (places - fixed + turn * (used - fixed)) % max(1, number_of - fixed)
        return jnp.zeros((number_of,), jnp.int32).at[ranking[jnp.where(places < fixed, places, shifted)]].set(jnp.asarray(tallies, jnp.int32))

    tallies = jnp.where(number % 4 == 0, named(heavy_load, number // 4), named(common, number - number // 4 - 1))
    mixed = jax.random.permutation(jax.random.fold_in(own, 3), number_of)
    donor, receiver = mixed[0:number_of // 2 * 2:2], mixed[1:number_of // 2 * 2:2]
    room = jnp.minimum(tallies[donor] - 1, most - tallies[receiver]) // 2
    room = jnp.where((donor == ranking[0]) | (receiver == ranking[0]) | (tallies[receiver] == 0), 0, jnp.maximum(room, 0))
    shifted = jax.random.randint(jax.random.fold_in(own, 4), (number_of // 2,), 0, 1 << 20) % (room + 1)
    tallies = tallies.at[donor].add(-shifted).at[receiver].add(shifted)
    members = jnp.searchsorted(jnp.cumsum(tallies), jnp.arange(rows * top), side="right").astype(jnp.int32)
    table = members.reshape(top, rows).T
    table = table[jax.random.permutation(jax.random.fold_in(own, 1), rows)]
    turn = jax.random.randint(jax.random.fold_in(own, 2), (rows, 1), 0, top)
    return jnp.take_along_axis(table, (jnp.arange(top)[None, :] + turn) % top, axis=1)


def portions_of(count, total, most, skew, full):
    weights = [(1 << 20) // math.isqrt(rank ** skew) + 1 for rank in range(1, count + 1)]
    largest = most if full else min(most, max(-(-total // count), total * weights[0] // sum(weights)))
    least = 1 if total - largest >= count - 1 else 0
    counts, rest = [largest] + [least] * (count - 1), total - largest - least * (count - 1)
    while rest > 0:
        candidates = [i for i in range(1, count) if counts[i] < largest] or [i for i in range(1, count) if counts[i] < most]
        mass, budget = sum([weights[i] for i in candidates]), rest
        for i in candidates:
            more = min(most - counts[i], max(1, budget * weights[i] // mass), rest)
            counts[i] = counts[i] + more
            rest = rest - more
    return np.array(counts)


def setup_inputs(seed: int = 0) -> dict:
    arg_keys = jax.random.split(jax.random.key(seed), 8)
    queries = draw_queries(jax.random.fold_in(arg_keys[7], 71), 0)
    documents = draw_documents(jax.random.fold_in(arg_keys[7], 71), 0)
    positives = draw_positives(jax.random.fold_in(arg_keys[7], 71), 0)
    inner_owner_keys = jax.random.split(jax.random.fold_in(arg_keys[3], 1), N_GRP * (N_DP * Q_DEV) // Q_DEV)
    inner_owner_turns = jax.random.permutation(jax.random.fold_in(arg_keys[3], 3), N_GRP * (N_DP * Q_DEV) // Q_DEV)
    inner_owner = jax.vmap(lambda own, number: deal_out(jax.random.fold_in(arg_keys[3], 2), own, number, Q_DEV, N_DP, 1, CAP_IN, 2))(inner_owner_keys, inner_owner_turns).reshape((N_GRP, N_DP * Q_DEV, 1))
    inner_row = touch_ends(jax.random.randint(arg_keys[4], (N_GRP, N_DP * Q_DEV, 1), 0, Q_DEV), jax.random.fold_in(arg_keys[4], 1), 0, Q_DEV - 1).astype(jnp.int32)
    outer_owner_keys = jax.random.split(jax.random.fold_in(arg_keys[5], 1), N_DP * N_GRP * Q_DEV // Q_DEV)
    outer_owner_turns = jax.random.permutation(jax.random.fold_in(arg_keys[5], 3), N_DP * N_GRP * Q_DEV // Q_DEV)
    outer_owner = jax.vmap(lambda own, number: deal_out(jax.random.fold_in(arg_keys[5], 2), own, number, Q_DEV, N_GRP - 1, 1, CAP_OUT, 2))(outer_owner_keys, outer_owner_turns).reshape((N_DP, N_GRP, Q_DEV, 1))
    outer_row = touch_ends(jax.random.randint(arg_keys[6], (N_DP, N_GRP, Q_DEV, 1), 0, Q_DEV), jax.random.fold_in(arg_keys[6], 1), 0, Q_DEV - 1).astype(jnp.int32)
    return dict(queries=queries, documents=documents, positives=positives, inner_owner=inner_owner, inner_row=inner_row, outer_owner=outer_owner, outer_row=outer_row)


def reference(queries, documents, positives, inner_owner, inner_row, outer_owner, outer_row):
    device_total = N_GRP * N_DP

    def one_device(gradient_total, device):
        group = device // N_DP
        column = device % N_DP
        start = device * Q_DEV
        q_block = lax.dynamic_slice_in_dim(queries, start, Q_DEV, 0)
        d_block = lax.dynamic_slice_in_dim(documents, start, Q_DEV, 0)
        inner_own = lax.dynamic_slice_in_dim(lax.dynamic_index_in_dim(inner_owner, group, 0, keepdims=False)[:, 0], column * Q_DEV, Q_DEV, 0)
        inner_at = lax.dynamic_slice_in_dim(lax.dynamic_index_in_dim(inner_row, group, 0, keepdims=False)[:, 0], column * Q_DEV, Q_DEV, 0)
        outer_col = lax.dynamic_index_in_dim(outer_owner, column, 0, keepdims=False)
        outer_own = lax.dynamic_index_in_dim(outer_col, group, 0, keepdims=False)[:, 0]
        outer_rcol = lax.dynamic_index_in_dim(outer_row, column, 0, keepdims=False)
        outer_at = lax.dynamic_index_in_dim(outer_rcol, group, 0, keepdims=False)[:, 0]
        inner_index = (group * N_DP + inner_own) * Q_DEV + inner_at
        target_group = (group + 1 + outer_own) % N_GRP
        outer_index = (target_group * N_DP + column) * Q_DEV + outer_at
        pool_index = jnp.concatenate([inner_index, outer_index]).astype(jnp.int32)
        pool_rows = jnp.take(documents, pool_index, axis=0)
        keys_all = jnp.concatenate([d_block, pool_rows], axis=0)
        scores = 3.0 * jnp.dot(q_block, keys_all.T, preferred_element_type=jnp.float32)
        row_max = jnp.max(scores, axis=1, keepdims=True)
        exp_scores = jnp.exp(scores - row_max)
        row_total = jnp.sum(exp_scores, axis=1, keepdims=True)
        pos_block = lax.dynamic_slice_in_dim(positives, start, Q_DEV, 0)
        column_ids = jnp.arange(3 * Q_DEV, dtype=jnp.int32)
        target = (column_ids[None, :] == pos_block[:, None]).astype(jnp.float32)
        pos_score = jnp.take_along_axis(scores, pos_block[:, None], axis=1)[:, 0]
        losses = row_max[:, 0] + jnp.log(row_total[:, 0]) - pos_score
        weights = (3.0 * (exp_scores / row_total - target)).astype(jnp.bfloat16)
        query_grads = jnp.dot(weights, keys_all, preferred_element_type=jnp.float32).astype(jnp.bfloat16)
        local_term = jnp.dot(weights[:, :Q_DEV].T, q_block, preferred_element_type=jnp.float32)
        slot_terms = jnp.dot(weights[:, Q_DEV:].T, q_block, preferred_element_type=jnp.float32).astype(jnp.bfloat16)
        slot_terms = lax.optimization_barrier(slot_terms).astype(jnp.float32)
        gradient_total = gradient_total.at[pool_index].add(slot_terms)
        current = lax.dynamic_slice_in_dim(gradient_total, start, Q_DEV, 0)
        gradient_total = lax.dynamic_update_slice_in_dim(gradient_total, current + local_term, start, 0)
        return gradient_total, (losses, query_grads)

    start_sum = jnp.zeros((TOKENS, D), jnp.float32)
    gradient_total, (losses, query_grads) = lax.scan(one_device, start_sum, jnp.arange(device_total, dtype=jnp.int32))
    return losses.reshape(TOKENS), query_grads.reshape(TOKENS, D), gradient_total.astype(jnp.bfloat16)
```

```python
import functools

import jax
import jax.numpy as jnp
from jax import lax
from jax.experimental import pallas as pl
from jax.experimental.pallas import tpu as pltpu
from jax.sharding import PartitionSpec as P

SPLIT = 4
SCALE = 3.0
VMEM = pl.BlockSpec(memory_space=pltpu.VMEM)
f32, bf16, i32 = jnp.float32, jnp.bfloat16, jnp.int32


def call(kernel, out_shape, *args, scratch=(), flops=0):
    nbytes = sum(a.size * a.dtype.itemsize for a in (*args, *jax.tree.leaves(out_shape)))
    return pl.pallas_call(
        kernel,
        out_shape=out_shape,
        in_specs=[VMEM] * len(args),
        out_specs=jax.tree.map(lambda _: VMEM, out_shape),
        scratch_shapes=list(scratch),
        compiler_params=pltpu.CompilerParams(vmem_limit_bytes=32 * 2**20),
        cost_estimate=pl.CostEstimate(flops=flops, bytes_accessed=nbytes, transcendentals=0),
    )(*args)


def dot(a, b, dims=((1,), (0,))):
    return lax.dot_general(a, b, (dims, ((), ())), preferred_element_type=f32)


NT = ((1,), (1,))
TN = ((0,), (0,))


def row_plan(count, split):
    t = lax.broadcasted_iota(i32, (count * split, 128), 0)
    chunk = jnp.zeros_like(t)
    for c in range(1, split):
        chunk = chunk + (t >= c * count).astype(i32)
    return t - count * chunk, chunk


def stacked(ref, split):
    width = ref.shape[1] // split
    return jnp.concatenate([ref[:, c * width : (c + 1) * width] for c in range(split)], axis=0)


def spread(values, chunk, split):
    return jnp.concatenate([jnp.where(chunk == c, values, 0.0).astype(bf16) for c in range(split)], axis=1)


def slot_codes(owner_ref, codes, axis, relative):
    peers, rows = owner_ref.shape
    me = lax.axis_index(axis)
    if relative:
        name = lax.rem(me - lax.broadcasted_iota(i32, (peers, rows), 0) - 1 + 2 * peers, peers)
    else:
        name = me
    wanted = owner_ref[...] == name
    earlier = lax.broadcasted_iota(i32, (rows, rows), 0) < lax.broadcasted_iota(i32, (rows, rows), 1)
    rank = dot(wanted.astype(f32).astype(bf16), earlier.astype(f32).astype(bf16))
    codes[...] = jnp.where(wanted, rank, -1.0).astype(i32)


def slot_onehot(codes, row_ref, axis, shift, slot):
    peers = codes.shape[0]
    r = lax.rem(lax.axis_index(axis) + shift, peers)
    chosen = codes[pl.ds(r, 1), :] == slot
    at = jnp.sum(jnp.where(chosen, row_ref[pl.ds(r, 1), :] + 1, 0).astype(f32), axis=1, keepdims=True)
    ids = lax.broadcasted_iota(i32, slot.shape, 1) + 1
    return jnp.where(ids.astype(f32) == at, 1.0, 0.0)


def send_kernel(axis, relative, shifts, count, split, owner_ref, row_ref, docs_ref, *refs):
    *outs, codes = refs
    slot_codes(owner_ref, codes, axis, relative)
    slot, chunk = row_plan(count, split)
    docs = stacked(docs_ref, split)
    for shift, out in zip(shifts, outs):
        onehot = slot_onehot(codes, row_ref, axis, shift, slot)
        out[...] = dot(spread(onehot, chunk, split), docs).astype(bf16)


def live_count(owner_ref, me, name):
    hit = (owner_ref[pl.ds(me, 1), :] == name).astype(f32)
    return jnp.sum(hit, axis=1, keepdims=True).astype(i32)


def near_kernel(shifts, q_ref, docs_ref, owner_ref, row_ref, *refs):
    *blocks, own_out, mult_out, inner_out = refs
    peers = owner_ref.shape[0]
    me = lax.axis_index("dp")
    q = q_ref[...]
    own_out[...] = SCALE * dot(docs_ref[...], q, NT)
    rows = docs_ref.shape[0]
    named = (owner_ref[pl.ds(me, 1), :] == me) & (
        row_ref[pl.ds(me, 1), :] == lax.broadcasted_iota(i32, (rows, rows), 0)
    )
    mult = jnp.sum(named.astype(f32), axis=1, keepdims=True)
    mult_out[...] = jnp.broadcast_to(mult, (rows, rows))
    count = blocks[0].shape[0]
    for n, (shift, block) in enumerate(zip(shifts, blocks)):
        live = live_count(owner_ref, me, lax.rem(me - shift + peers, peers))
        scores = SCALE * dot(block[...], q, NT)
        slot = lax.broadcasted_iota(i32, scores.shape, 0)
        inner_out[n * count : (n + 1) * count, :] = jnp.where(slot < live, scores, -jnp.inf)


def main_kernel(shifts, count, split, q_ref, own_ref, mult_ref, inner_ref, pos_ref, owner_ref, *refs):
    nseg = len(shifts)
    blocks, refs = refs[:nseg], refs[nseg:]
    loss_out, own_w, inner_w, outer_w = refs[:4]
    grads = refs[4 : 4 + nseg]
    acc = refs[-1]
    peers = owner_ref.shape[0]
    me = lax.axis_index("grp")
    slot, chunk = row_plan(count, split)
    width = q_ref.shape[1] // split
    own, inner = own_ref[...], inner_ref[...]
    top = jnp.maximum(jnp.max(own, axis=0, keepdims=True), jnp.max(inner, axis=0, keepdims=True))
    size = count * split
    for n, (shift, block) in enumerate(zip(shifts, blocks)):
        part = jnp.zeros(slot.shape, f32)
        for c in range(split):
            part = jnp.where(chunk == c, dot(block[...], q_ref[:, c * width : (c + 1) * width], NT), part)
        scores = part
        for c in range(1, split):
            scores = scores + pltpu.roll(part, c * count, 0)
        live = live_count(owner_ref, me, peers - 1 - shift)
        scores = jnp.where(slot < live, SCALE * scores, -jnp.inf)
        acc[n * size : (n + 1) * size, :] = scores
        top = jnp.maximum(top, jnp.max(scores, axis=0, keepdims=True))
    own_e = (1.0 + mult_ref[...]) * jnp.exp(own - top)
    inner_e = jnp.exp(inner - top)
    total = jnp.sum(own_e, axis=0, keepdims=True) + jnp.sum(inner_e, axis=0, keepdims=True)
    for n in range(nseg):
        e = jnp.exp(acc[n * size : (n + 1) * size, :] - top)
        acc[n * size : (n + 1) * size, :] = e
        total = total + jnp.sum(jnp.where(chunk == 0, e, 0.0), axis=0, keepdims=True)
    factor = SCALE / total
    q = stacked(q_ref, split)
    for n in range(nseg):
        w = acc[n * size : (n + 1) * size, :] * factor
        outer_w[n * size : (n + 1) * size, :] = w.astype(bf16)
        grads[n][...] = dot(spread(w, chunk, split), q).astype(bf16)
    positive = (lax.broadcasted_iota(i32, own.shape, 0) == pos_ref[...]).astype(f32)
    loss_out[...] = top + jnp.log(total) - jnp.sum(positive * own, axis=0, keepdims=True)
    own_w[...] = (own_e * factor - SCALE * positive).astype(bf16)
    inner_w[...] = (inner_e * factor).astype(bf16)


def inner_grad_kernel(w_ref, q_ref, *outs):
    count = outs[0].shape[0]
    for n, out in enumerate(outs):
        out[...] = dot(w_ref[n * count : (n + 1) * count, :], q_ref[...]).astype(bf16)


def query_grad_kernel(n_inner, count, split, own_w, inner_w, outer_w, docs_ref, *refs):
    *blocks, out = refs
    inner, outer = blocks[:n_inner], blocks[n_inner:]
    _, chunk = row_plan(count, split)
    width = docs_ref.shape[1] // split
    size = count * split
    cap = inner[0].shape[0]
    for c in range(split):
        cols = slice(c * width, (c + 1) * width)
        acc = dot(own_w[...], docs_ref[:, cols], TN)
        for n, block in enumerate(inner):
            acc = acc + dot(inner_w[n * cap : (n + 1) * cap, :], block[:, cols], TN)
        for n, block in enumerate(outer):
            w = outer_w[n * size : (n + 1) * size, :].astype(f32)
            acc = acc + dot(jnp.where(chunk == c, w, 0.0).astype(bf16), block[...], TN)
        out[:, cols] = acc.astype(bf16)


def near_grad_kernel(shifts, own_w, q_ref, owner_ref, row_ref, *refs):
    *blocks, out, codes = refs
    slot_codes(owner_ref, codes, "dp", False)
    slot = lax.broadcasted_iota(i32, (blocks[0].shape[0], 128), 0)
    onehots = [slot_onehot(codes, row_ref, "dp", shift, slot).astype(bf16) for shift in shifts]
    width = q_ref.shape[1] // SPLIT
    for c in range(SPLIT):
        cols = slice(c * width, (c + 1) * width)
        acc = dot(own_w[...], q_ref[:, cols])
        for onehot, block in zip(onehots, blocks):
            acc = acc + dot(onehot, block[:, cols], TN)
        out[:, cols] = acc


def far_grad_kernel(shifts, count, split, near_ref, owner_ref, row_ref, *refs):
    *blocks, out, codes = refs
    slot_codes(owner_ref, codes, "grp", True)
    slot, chunk = row_plan(count, split)
    onehots = [slot_onehot(codes, row_ref, "grp", shift, slot) for shift in shifts]
    width = near_ref.shape[1] // split
    for c in range(split):
        cols = slice(c * width, (c + 1) * width)
        acc = near_ref[:, cols]
        for onehot, block in zip(onehots, blocks):
            acc = acc + dot(jnp.where(chunk == c, onehot, 0.0).astype(bf16), block[...], TN)
        out[:, cols] = acc.astype(bf16)


def shifted(block, axis, shift):
    size = lax.axis_size(axis)
    return lax.ppermute(block, axis, [(g, (g + shift) % size) for g in range(size)])


def per_device(queries, documents, positives, inner_owner, inner_row, outer_owner, outer_row):
    rows, width = queries.shape
    dp, grp = lax.axis_size("dp"), lax.axis_size("grp")
    cap_inner = -(-max(2, 2 * rows // dp) // 16) * 16
    cap_outer = -(-max(2, 2 * rows // (grp - 1)) // 4) * 4
    shape = jax.ShapeDtypeStruct
    in_shifts = list(range(1, dp))
    out_shifts = sorted(range(1, grp), key=lambda k: (abs(2 * k - grp), k))
    inner_owner, inner_row = inner_owner.reshape(dp, rows), inner_row.reshape(dp, rows)
    outer_owner, outer_row = outer_owner.reshape(grp, rows), outer_row.reshape(grp, rows)
    outer_block = shape((cap_outer * SPLIT, width // SPLIT), bf16)
    inner_block = shape((cap_inner, width), bf16)
    n_in, n_out = len(in_shifts), len(out_shifts)

    send_outer = call(
        functools.partial(send_kernel, "grp", True, out_shifts, cap_outer, SPLIT),
        [outer_block] * n_out,
        outer_owner, outer_row, documents,
        scratch=[pltpu.VMEM((grp, rows), i32)],
        flops=2 * n_out * cap_outer * SPLIT * rows * width,
    )
    got_outer = [shifted(b, "grp", k) for b, k in zip(send_outer, out_shifts)]
    send_inner = call(
        functools.partial(send_kernel, "dp", False, in_shifts, cap_inner, 1),
        [inner_block] * n_in,
        inner_owner, inner_row, documents,
        scratch=[pltpu.VMEM((dp, rows), i32)],
        flops=2 * n_in * cap_inner * rows * width,
    )
    got_inner = [shifted(b, "dp", k) for b, k in zip(send_inner, in_shifts)]
    own_scores, mult, inner_scores = call(
        functools.partial(near_kernel, in_shifts),
        [shape((rows, rows), f32), shape((rows, rows), f32), shape((n_in * cap_inner, rows), f32)],
        queries, documents, inner_owner, inner_row, *got_inner,
        flops=2 * (n_in * cap_inner + rows) * rows * width,
    )
    losses, own_w, inner_w, outer_w, *grads_outer = call(
        functools.partial(main_kernel, out_shifts, cap_outer, SPLIT),
        [
            shape((1, rows), f32),
            shape((rows, rows), bf16),
            shape((n_in * cap_inner, rows), bf16),
            shape((n_out * cap_outer * SPLIT, rows), bf16),
        ]
        + [outer_block] * n_out,
        queries, own_scores, mult, inner_scores, positives.reshape(1, rows), outer_owner, *got_outer,
        scratch=[pltpu.VMEM((n_out * cap_outer * SPLIT, rows), f32)],
        flops=4 * n_out * cap_outer * SPLIT * rows * width,
    )
    back_outer = [shifted(b, "grp", -k) for b, k in zip(grads_outer, out_shifts)]
    grads_inner = call(
        inner_grad_kernel, [inner_block] * n_in, inner_w, queries, flops=2 * n_in * cap_inner * rows * width
    )
    back_inner = [shifted(b, "dp", -k) for b, k in zip(grads_inner, in_shifts)]
    query_grads = call(
        functools.partial(query_grad_kernel, n_in, cap_outer, SPLIT),
        shape((rows, width), bf16),
        own_w, inner_w, outer_w, documents, *got_inner, *got_outer,
        flops=2 * (n_out * cap_outer * SPLIT + n_in * cap_inner + rows) * rows * width,
    )
    near_grads = call(
        functools.partial(near_grad_kernel, in_shifts),
        shape((rows, width), f32),
        own_w, queries, inner_owner, inner_row, *back_inner,
        scratch=[pltpu.VMEM((dp, rows), i32)],
        flops=2 * (n_in * cap_inner + rows) * rows * width,
    )
    doc_grads = call(
        functools.partial(far_grad_kernel, out_shifts, cap_outer, SPLIT),
        shape((rows, width), bf16),
        near_grads, outer_owner, outer_row, *back_outer,
        scratch=[pltpu.VMEM((grp, rows), i32)],
        flops=2 * n_out * cap_outer * SPLIT * rows * width,
    )
    return losses.reshape(rows), query_grads, doc_grads


def solution(mesh):
    return jax.shard_map(
        per_device,
        mesh=mesh,
        in_specs=(
            P(("grp", "dp"), None),
            P(("grp", "dp"), None),
            P(("grp", "dp")),
            P("grp", None, None),
            P("grp", None, None),
            P("dp", None, None, None),
            P("dp", None, None, None),
        ),
        out_specs=(P(("grp", "dp")), P(("grp", "dp"), None), P(("grp", "dp"), None)),
        check_vma=False,
    )
```

```python
import functools

import jax
import jax.numpy as jnp
from jax import lax
from jax.experimental import pallas as pl
from jax.experimental.pallas import tpu as pltpu
from jax.sharding import PartitionSpec as P

SPLIT = 4
SCALE = 3.0
VMEM = pl.BlockSpec(memory_space=pltpu.VMEM)
f32, bf16, i32 = jnp.float32, jnp.bfloat16, jnp.int32


ANY = pl.BlockSpec(memory_space=pl.ANY)


def call(kernel, out_shape, *args, scratch=(), flops=0, in_space=VMEM, out_space=VMEM):
    nbytes = sum(a.size * a.dtype.itemsize for a in (*args, *jax.tree.leaves(out_shape)))
    return pl.pallas_call(
        kernel,
        out_shape=out_shape,
        in_specs=[in_space] * len(args),
        out_specs=jax.tree.map(lambda _: out_space, out_shape),
        scratch_shapes=list(scratch),
        compiler_params=pltpu.CompilerParams(vmem_limit_bytes=32 * 2**20),
        cost_estimate=pl.CostEstimate(flops=flops, bytes_accessed=nbytes, transcendentals=0),
    )(*args)


def dot(a, b, dims=((1,), (0,))):
    return lax.dot_general(a, b, (dims, ((), ())), preferred_element_type=f32)


NT = ((1,), (1,))
TN = ((0,), (0,))


def row_plan(segment):
    _, first, count = segment
    t = lax.broadcasted_iota(i32, (count * SPLIT, 128), 0)
    chunk = jnp.zeros_like(t)
    for c in range(1, SPLIT):
        chunk = chunk + (t >= c * count).astype(i32)
    return t - count * chunk + first, chunk


def stacked(ref):
    width = ref.shape[1] // SPLIT
    return jnp.concatenate([ref[:, c * width : (c + 1) * width] for c in range(SPLIT)], axis=0)


def spread(values, chunk):
    return jnp.concatenate([jnp.where(chunk == c, values, 0.0).astype(bf16) for c in range(SPLIT)], axis=1)


def slot_codes(owner_ref, codes):
    peers, rows = owner_ref.shape
    me = lax.axis_index("grp")
    name = lax.rem(me - lax.broadcasted_iota(i32, (peers, rows), 0) - 1 + 2 * peers, peers)
    wanted = owner_ref[...] == name
    earlier = lax.broadcasted_iota(i32, (rows, rows), 0) < lax.broadcasted_iota(i32, (rows, rows), 1)
    rank = dot(wanted.astype(f32).astype(bf16), earlier.astype(f32).astype(bf16))
    codes[...] = jnp.where(wanted, rank, -1.0).astype(i32)


def slot_onehot(codes, row_ref, shift, slot):
    r = lax.rem(lax.axis_index("grp") + shift, codes.shape[0])
    chosen = codes[pl.ds(r, 1), :] == slot
    at = jnp.sum(jnp.where(chosen, row_ref[pl.ds(r, 1), :] + 1, 0).astype(f32), axis=1, keepdims=True)
    ids = lax.broadcasted_iota(i32, slot.shape, 1) + 1
    return jnp.where(ids.astype(f32) == at, 1.0, 0.0)


def send_kernel(segments, owner_hbm, row_hbm, docs_hbm, *refs):
    *outs, codes, owner_ref, row_ref, docs_ref, sems = refs
    copies = [
        pltpu.make_async_copy(src, dst, sems.at[n])
        for n, (src, dst) in enumerate(((owner_hbm, owner_ref), (row_hbm, row_ref), (docs_hbm, docs_ref)))
    ]
    for copy in copies:
        copy.start()
    for copy in copies:
        copy.wait()
    slot_codes(owner_ref, codes)
    docs = stacked(docs_ref)
    for segment, out in zip(segments, outs):
        slot, chunk = row_plan(segment)
        onehot = slot_onehot(codes, row_ref, segment[0], slot)
        out[...] = dot(spread(onehot, chunk), docs).astype(bf16)


def subset_kernel(shifts, base, owner_ref, out):
    index = jnp.int32(0)
    for n, shift in enumerate(shifts):
        hits = (owner_ref[...] == owner_ref.shape[0] - 1 - shift).astype(f32)
        most = jnp.max(jnp.sum(hits, axis=1, keepdims=True))
        index = index + jnp.where(most > base, 1 << n, 0).astype(i32)
    out[0, 0] = index


def live_count(owner_ref, shift):
    hit = owner_ref[pl.ds(lax.axis_index("grp"), 1), :] == owner_ref.shape[0] - 1 - shift
    return jnp.sum(hit.astype(f32), axis=1, keepdims=True).astype(i32)


def near_kernel(q_ref, owner_ref, row_ref, docs_ref, scores_out, times_out):
    me = lax.axis_index("dp")
    rows = q_ref.shape[0]
    owner, row = owner_ref[pl.ds(me, 1), :], row_ref[pl.ds(me, 1), :]
    same_row = row == lax.broadcasted_iota(i32, (rows, rows), 0)
    for d in range(owner_ref.shape[0]):
        part = slice(d * rows, (d + 1) * rows)
        times = jnp.sum((same_row & (owner == d)).astype(f32), axis=1, keepdims=True)
        times = jnp.broadcast_to(times + jnp.where(me == d, 1.0, 0.0), (rows, rows))
        scores = SCALE * dot(docs_ref[part, :], q_ref[...], NT)
        times_out[part, :] = times
        scores_out[part, :] = jnp.where(times > 0.0, scores, -jnp.inf)


def main_kernel(segments, q_ref, near_ref, times_ref, pos_ref, owner_ref, *refs):
    nseg = len(segments)
    blocks, refs = refs[:nseg], refs[nseg:]
    loss_out, near_w, *refs = refs
    far_w, grads, acc = refs[:nseg], refs[nseg:-1], refs[-1]
    rows = q_ref.shape[0]
    width = q_ref.shape[1] // SPLIT
    near = near_ref[...]
    top = jnp.max(near, axis=0, keepdims=True)
    start = 0
    for segment, block in zip(segments, blocks):
        slot, chunk = row_plan(segment)
        part = jnp.zeros(slot.shape, f32)
        for c in range(SPLIT):
            part = jnp.where(chunk == c, dot(block[...], q_ref[:, c * width : (c + 1) * width], NT), part)
        scores = part
        for c in range(1, SPLIT):
            scores = scores + pltpu.roll(part, c * segment[2], 0)
        scores = jnp.where(slot < live_count(owner_ref, segment[0]), SCALE * scores, -jnp.inf)
        acc[start : start + block.shape[0], :] = scores
        start += block.shape[0]
        top = jnp.maximum(top, jnp.max(scores, axis=0, keepdims=True))
    near_e = times_ref[...] * jnp.exp(near - top)
    total = jnp.sum(near_e, axis=0, keepdims=True)
    start = 0
    for segment, block in zip(segments, blocks):
        _, chunk = row_plan(segment)
        e = jnp.exp(acc[start : start + block.shape[0], :] - top)
        acc[start : start + block.shape[0], :] = e
        start += block.shape[0]
        total = total + jnp.sum(jnp.where(chunk == 0, e, 0.0), axis=0, keepdims=True)
    factor = SCALE / total
    q = stacked(q_ref)
    start = 0
    for segment, w_out, out in zip(segments, far_w, grads):
        _, chunk = row_plan(segment)
        w = acc[start : start + out.shape[0], :] * factor
        start += out.shape[0]
        w_out[...] = w.astype(bf16)
        out[...] = dot(spread(w, chunk), q).astype(bf16)
    own = lax.axis_index("dp") * rows
    positive = (lax.broadcasted_iota(i32, near.shape, 0) == pos_ref[...] + own).astype(f32)
    loss_out[...] = top + jnp.log(total) - jnp.sum(jnp.where(positive > 0.0, near, 0.0), axis=0, keepdims=True)
    near_w[...] = (near_e * factor - SCALE * positive).astype(bf16)


def query_grad_kernel(segments, near_w, docs_ref, *refs):
    nseg = len(segments)
    *refs, out = refs
    far_w, far = refs[:nseg], refs[nseg:]
    width = out.shape[1] // SPLIT
    for c in range(SPLIT):
        cols = slice(c * width, (c + 1) * width)
        acc = dot(near_w[...], docs_ref[:, cols], TN)
        for segment, w, block in zip(segments, far_w, far):
            _, chunk = row_plan(segment)
            acc = acc + dot(jnp.where(chunk == c, w[...].astype(f32), 0.0).astype(bf16), block[...], TN)
        out[:, cols] = acc.astype(bf16)


def near_grad_kernel(weights, q_ref, out):
    rows = out.shape[0]
    width = out.shape[1] // SPLIT
    for c in range(SPLIT):
        cols = slice(c * width, (c + 1) * width)
        acc = jnp.zeros((rows, width), f32)
        for d in range(weights.shape[0] // rows):
            part = slice(d * rows, (d + 1) * rows)
            acc = acc + dot(weights[part, :], q_ref[part, cols])
        out[:, cols] = acc


def far_grad_kernel(segments, near_ref, owner_ref, row_ref, *refs):
    *blocks, out, codes = refs
    slot_codes(owner_ref, codes)
    plans = [row_plan(segment) for segment in segments]
    onehots = [slot_onehot(codes, row_ref, s[0], slot) for s, (slot, _) in zip(segments, plans)]
    width = out.shape[1] // SPLIT
    for c in range(SPLIT):
        cols = slice(c * width, (c + 1) * width)
        acc = near_ref[:, cols]
        for onehot, (_, chunk), block in zip(onehots, plans, blocks):
            acc = acc + dot(jnp.where(chunk == c, onehot, 0.0).astype(bf16), block[...], TN)
        out[:, cols] = acc.astype(bf16)


def shifted(block, shift):
    size = lax.axis_size("grp")
    return lax.ppermute(block, "grp", [(g, (g + shift) % size) for g in range(size)])


def after(value, *others):
    return lax.optimization_barrier((value, *others))[0]


def exchange(blocks, segments, split_shifts, index, sign):
    base = {s[0]: b for s, b in zip(segments, blocks) if s[1] == 0}
    more = {s[0]: b for s, b in zip(segments, blocks) if s[1] > 0}
    got = {}
    if not more:
        return [shifted(base[s[0]], sign * s[0]) for s in segments]
    heads, pilot = list(base)[:3], list(base)[-2:]
    for k in [*heads, pilot[0]]:
        got[k] = shifted(base[k], sign * k)
    extra, token = {}, got[pilot[0]]
    for bit, k in enumerate(split_shifts):
        wanted = lax.bitwise_and(lax.shift_right_logical(index, bit), 1) > 0
        extra[k] = token = lax.cond(wanted, lambda b, k=k: shifted(b, sign * k), lambda b: b, after(more[k], token))
    for k, token in zip([k for k in base if k not in got], [got[heads[0]], got[heads[1]], token]):
        got[k] = shifted(after(base[k], token), sign * k)
    return [got[s[0]] if s[1] == 0 else extra[s[0]] for s in segments]


def per_device(queries, documents, positives, inner_owner, inner_row, outer_owner, outer_row):
    rows, width = queries.shape
    dp, grp = lax.axis_size("dp"), lax.axis_size("grp")
    cap = -(-max(2, 2 * rows // (grp - 1)) // 4) * 4
    base = -(-2 * cap // 12) * 4
    shape = jax.ShapeDtypeStruct
    shifts = sorted(range(1, grp), key=lambda k: (abs(2 * k - grp), k))
    split_shifts = [k for k in shifts if 1 < k < grp - 1] if grp <= 8 else []
    segments = [(k, 0, base if k in split_shifts else cap) for k in shifts] + [(k, base, cap - base) for k in split_shifts]
    inner_owner, inner_row = inner_owner.reshape(dp, rows), inner_row.reshape(dp, rows)
    outer_owner, outer_row = outer_owner.reshape(grp, rows), outer_row.reshape(grp, rows)
    far_blocks = [shape((s[2] * SPLIT, width // SPLIT), bf16) for s in segments]
    far_rows = sum(b.shape[0] for b in far_blocks)
    far_flops, near_flops = 2 * far_rows * rows * width, 2 * dp * rows * rows * width

    send = call(
        functools.partial(send_kernel, segments),
        far_blocks,
        outer_owner, outer_row, documents,
        scratch=[
            pltpu.VMEM((grp, rows), i32),
            pltpu.VMEM((grp, rows), i32),
            pltpu.VMEM((grp, rows), i32),
            pltpu.VMEM((rows, width), bf16),
            pltpu.SemaphoreType.DMA((3,)),
        ],
        flops=far_flops,
        in_space=ANY,
    )
    subset = call(
        functools.partial(subset_kernel, split_shifts, base),
        shape((1, 1), i32),
        after(outer_owner, send[0]),
        out_space=pl.BlockSpec(memory_space=pltpu.SMEM),
    )[0, 0]
    got = exchange(send, segments, split_shifts, subset, 1)
    docs = lax.all_gather(after(documents, send[0]), "dp", axis=0, tiled=True)
    scores, times = call(
        near_kernel,
        [shape((dp * rows, rows), f32)] * 2,
        queries, inner_owner, inner_row, docs,
        flops=near_flops,
    )
    far_weights = [shape((b.shape[0], rows), bf16) for b in far_blocks]
    losses, *out = call(
        functools.partial(main_kernel, segments),
        [shape((1, rows), f32), shape((dp * rows, rows), bf16)] + far_weights + far_blocks,
        queries, scores, times, positives.reshape(1, rows), outer_owner, *got,
        scratch=[pltpu.VMEM((far_rows, rows), f32)],
        flops=2 * far_flops,
    )
    near_w, far_w, far_grads = out[0], out[1 : 1 + len(segments)], out[1 + len(segments) :]
    back = exchange(far_grads, segments, split_shifts, subset, -1)
    query_grads = call(
        functools.partial(query_grad_kernel, segments),
        shape((rows, width), bf16),
        near_w, docs, *far_w, *got,
        flops=far_flops + near_flops,
    )
    owned_w = lax.all_to_all(after(near_w, query_grads), "dp", split_axis=0, concat_axis=0, tiled=True)
    all_queries = lax.all_gather(after(queries, losses), "dp", axis=0, tiled=True)
    near_grads = call(near_grad_kernel, shape((rows, width), f32), owned_w, all_queries, flops=near_flops)
    doc_grads = call(
        functools.partial(far_grad_kernel, segments),
        shape((rows, width), bf16),
        near_grads, outer_owner, outer_row, *back,
        scratch=[pltpu.VMEM((grp, rows), i32)],
        flops=far_flops,
    )
    return losses.reshape(rows), query_grads, doc_grads


def solution(mesh):
    return jax.shard_map(
        per_device,
        mesh=mesh,
        in_specs=(
            P(("grp", "dp"), None),
            P(("grp", "dp"), None),
            P(("grp", "dp")),
            P("grp", None, None),
            P("grp", None, None),
            P("dp", None, None, None),
            P("dp", None, None, None),
        ),
        out_specs=(P(("grp", "dp")), P(("grp", "dp"), None), P(("grp", "dp"), None)),
        check_vma=False,
    )
```

```python
import functools

import jax
import jax.numpy as jnp
from jax import lax
from jax.experimental import pallas as pl
from jax.experimental.pallas import tpu as pltpu
from jax.sharding import PartitionSpec as P

COLUMNS = 4
SCALE = 3.0
VMEM = pl.BlockSpec(memory_space=pltpu.VMEM)
f32, bf16, i32 = jnp.float32, jnp.bfloat16, jnp.int32


ANY = pl.BlockSpec(memory_space=pl.ANY)


def call(kernel, out_shape, *args, scratch=(), flops=0, in_space=VMEM, out_space=VMEM, vmem=24):
    nbytes = sum(a.size * a.dtype.itemsize for a in (*args, *jax.tree.leaves(out_shape)))
    return pl.pallas_call(
        kernel,
        out_shape=out_shape,
        in_specs=in_space if isinstance(in_space, list) else [in_space] * len(args),
        out_specs=jax.tree.map(lambda _: out_space, out_shape),
        scratch_shapes=list(scratch),
        compiler_params=pltpu.CompilerParams(vmem_limit_bytes=vmem * 2**20),
        cost_estimate=pl.CostEstimate(flops=flops, bytes_accessed=nbytes, transcendentals=0),
    )(*args)


def dot(a, b, dims=((1,), (0,))):
    return lax.dot_general(a, b, (dims, ((), ())), preferred_element_type=f32)


NT = ((1,), (1,))
TN = ((0,), (0,))


def row_plan(segments, split):
    slots, chunks = [], []
    for _, first, count in segments:
        t = lax.broadcasted_iota(i32, (count * split, 128), 0)
        chunk = jnp.zeros_like(t)
        for c in range(1, split):
            chunk = chunk + (t >= c * count).astype(i32)
        slots.append(t - count * chunk + first)
        chunks.append(chunk)
    return jnp.concatenate(slots, axis=0), jnp.concatenate(chunks, axis=0)


def bounds(segments, split):
    ends = [0]
    for segment in segments:
        ends.append(ends[-1] + segment[2] * split)
    return list(zip(ends[:-1], ends[1:]))


def stacked(ref, split):
    width = ref.shape[1] // split
    return jnp.concatenate([ref[:, c * width : (c + 1) * width] for c in range(split)], axis=0)


def spread(values, chunk, split):
    if split == 1:
        return values.astype(bf16)
    return jnp.concatenate([jnp.where(chunk == c, values, 0.0).astype(bf16) for c in range(split)], axis=1)


def slot_codes(owner_ref, codes):
    peers, rows = owner_ref.shape
    me = lax.axis_index("grp")
    name = lax.rem(me - lax.broadcasted_iota(i32, (peers, rows), 0) - 1 + 2 * peers, peers)
    wanted = owner_ref[...] == name
    earlier = lax.broadcasted_iota(i32, (rows, rows), 0) < lax.broadcasted_iota(i32, (rows, rows), 1)
    rank = dot(wanted.astype(f32).astype(bf16), earlier.astype(f32).astype(bf16))
    codes[...] = jnp.where(wanted, rank, -1.0).astype(i32)


def slot_onehot(codes, row_ref, segments, split):
    slot, chunk = row_plan(segments, split)
    asked = []
    for (shift, _, _), (start, end) in zip(segments, bounds(segments, split)):
        r = lax.rem(lax.axis_index("grp") + shift, codes.shape[0])
        chosen = codes[pl.ds(r, 1), :] == slot[start:end]
        asked.append(jnp.where(chosen, row_ref[pl.ds(r, 1), :] + 1, 0).astype(f32))
    at = jnp.sum(jnp.concatenate(asked, axis=0), axis=1, keepdims=True)
    ids = lax.broadcasted_iota(i32, slot.shape, 1) + 1
    return jnp.where(ids.astype(f32) == at, 1.0, 0.0), chunk


def pick(items, groups):
    items = iter(items)
    return [[next(items) for _ in segments] for _, segments in groups]


def send_kernel(groups, owner_hbm, row_hbm, docs_hbm, *refs):
    *outs, codes, owner_ref, row_ref, docs_ref, sems = refs
    copies = [
        pltpu.make_async_copy(src, dst, sems.at[n])
        for n, (src, dst) in enumerate(((owner_hbm, owner_ref), (row_hbm, row_ref), (docs_hbm, docs_ref)))
    ]
    for copy in copies:
        copy.start()
    for copy in copies:
        copy.wait()
    slot_codes(owner_ref, codes)
    for (split, segments), blocks in zip(groups, pick(outs, groups)):
        onehot, chunk = slot_onehot(codes, row_ref, segments, split)
        rows = dot(spread(onehot, chunk, split), stacked(docs_ref, split))
        for (start, end), out in zip(bounds(segments, split), blocks):
            out[...] = rows[start:end].astype(bf16)


def subset_kernel(shifts, base, owner_ref, _, out):
    index = jnp.int32(0)
    for n, shift in enumerate(shifts):
        hits = (owner_ref[...] == owner_ref.shape[0] - 1 - shift).astype(f32)
        most = jnp.max(jnp.sum(hits, axis=1, keepdims=True))
        index = index + jnp.where(most > base, 1 << n, 0).astype(i32)
    out[0, 0] = index


def later_kernel(index_ref, *refs):
    refs[-1][0, 0] = index_ref[0, 0]


def live_count(owner_ref, shift):
    hit = owner_ref[pl.ds(lax.axis_index("grp"), 1), :] == owner_ref.shape[0] - 1 - shift
    return jnp.sum(hit.astype(f32), axis=1, keepdims=True).astype(i32)


def near_kernel(q_ref, owner_ref, row_ref, docs_ref, scores_out, times_out):
    me = lax.axis_index("dp")
    rows = q_ref.shape[0]
    owner, row = owner_ref[pl.ds(me, 1), :], row_ref[pl.ds(me, 1), :]
    same_row = row == lax.broadcasted_iota(i32, (rows, rows), 0)
    for d in range(owner_ref.shape[0]):
        part = slice(d * rows, (d + 1) * rows)
        times = jnp.sum((same_row & (owner == d)).astype(f32), axis=1, keepdims=True)
        times = jnp.broadcast_to(times + jnp.where(me == d, 1.0, 0.0), (rows, rows))
        scores = SCALE * dot(docs_ref[part, :], q_ref[...], NT)
        times_out[part, :] = times
        scores_out[part, :] = jnp.where(times > 0.0, scores, -jnp.inf)


def main_kernel(groups, q_ref, near_ref, times_ref, pos_ref, owner_ref, *refs):
    nseg = sum(len(segments) for _, segments in groups)
    blocks, refs = pick(refs[:nseg], groups), refs[nseg:]
    loss_out, near_w, *refs = refs
    grads, refs = pick(refs[:nseg], groups), refs[nseg:]
    far_ws, fars = refs[: len(groups)], refs[len(groups) :]
    near = near_ref[...]
    top = jnp.max(near, axis=0, keepdims=True)
    all_scores = []
    for (split, segments), received, far in zip(groups, blocks, fars):
        slot, chunk = row_plan(segments, split)
        far[...] = jnp.concatenate([block[...] for block in received], axis=0)
        width = far.shape[1]
        part = dot(far[...], q_ref[:, :width], NT)
        for c in range(1, split):
            part = jnp.where(chunk == c, dot(far[...], q_ref[:, c * width : (c + 1) * width], NT), part)
        scores = []
        for segment, (start, end) in zip(segments, bounds(segments, split)):
            total = part[start:end]
            for c in range(1, split):
                total = total + pltpu.roll(part[start:end], c * segment[2], 0)
            live = live_count(owner_ref, segment[0])
            scores.append(jnp.where(slot[start:end] < live, SCALE * total, -jnp.inf))
        scores = jnp.concatenate(scores, axis=0)
        all_scores.append(scores)
        top = jnp.maximum(top, jnp.max(scores, axis=0, keepdims=True))
    near_e = times_ref[...] * jnp.exp(near - top)
    total = jnp.sum(near_e, axis=0, keepdims=True)
    all_e = []
    for (split, segments), scores in zip(groups, all_scores):
        _, chunk = row_plan(segments, split)
        e = jnp.exp(scores - top)
        all_e.append(e)
        total = total + jnp.sum(jnp.where(chunk == 0, e, 0.0), axis=0, keepdims=True)
    factor = SCALE / total
    for (split, segments), e, outs, far_w in zip(groups, all_e, grads, far_ws):
        _, chunk = row_plan(segments, split)
        w = e * factor
        far_w[...] = w.astype(bf16)
        rows = dot(spread(w, chunk, split), stacked(q_ref, split))
        for (start, end), out in zip(bounds(segments, split), outs):
            out[...] = rows[start:end].astype(bf16)
    own = lax.axis_index("dp") * q_ref.shape[0]
    positive = (lax.broadcasted_iota(i32, near.shape, 0) == pos_ref[...] + own).astype(f32)
    loss_out[...] = top + jnp.log(total) - jnp.sum(jnp.where(positive > 0.0, near, 0.0), axis=0, keepdims=True)
    near_w[...] = (near_e * factor - SCALE * positive).astype(bf16)


def add_groups(groups, selects, blocks, acc, cols):
    for (split, segments), select, block in zip(groups, selects, blocks):
        width = block.shape[1]
        chunk = cols.start // width
        if split > 1:
            select = jnp.where(row_plan(segments, split)[1] == chunk, select, 0.0)
        acc = acc + dot(select.astype(bf16), block[:, cols.start - chunk * width : cols.stop - chunk * width], TN)
    return acc


def query_grad_kernel(groups, near_w, docs_ref, *refs):
    *refs, out = refs
    selects, blocks = [ref[...].astype(f32) for ref in refs[: len(groups)]], refs[len(groups) :]
    width = out.shape[1] // COLUMNS
    for c in range(COLUMNS):
        cols = slice(c * width, (c + 1) * width)
        acc = dot(near_w[...], docs_ref[:, cols], TN)
        out[:, cols] = add_groups(groups, selects, blocks, acc, cols).astype(bf16)


def near_grad_kernel(weights, q_ref, out):
    rows = out.shape[0]
    peers = q_ref.shape[0] // rows
    width = out.shape[1] // COLUMNS
    mine = lax.axis_index("dp") * rows
    mine = [weights[pl.ds(pl.multiple_of(d * peers * rows + mine, rows), rows), :] for d in range(peers)]
    mine = jnp.concatenate(mine, axis=1)
    for c in range(COLUMNS):
        cols = slice(c * width, (c + 1) * width)
        out[:, cols] = dot(mine, q_ref[:, cols])


def far_grad_kernel(groups, near_ref, owner_ref, row_ref, *refs):
    *refs, out, codes = refs
    slot_codes(owner_ref, codes)
    selects = [slot_onehot(codes, row_ref, segments, split)[0] for split, segments in groups]
    blocks = [jnp.concatenate([block[...] for block in received], axis=0) for received in pick(refs, groups)]
    width = out.shape[1] // COLUMNS
    for c in range(COLUMNS):
        cols = slice(c * width, (c + 1) * width)
        out[:, cols] = add_groups(groups, selects, blocks, near_ref[:, cols], cols).astype(bf16)


def shifted(block, shift):
    size = lax.axis_size("grp")
    return lax.ppermute(block, "grp", [(g, (g + shift) % size) for g in range(size)])


def exchange(blocks, segments, find_index, sign):
    base = {s[0]: b for s, b in zip(segments, blocks) if s[1] == 0}
    more = {s[0]: b for s, b in zip(segments, blocks) if s[1] > 0}
    if not more:
        return [shifted(base[s[0]], sign * s[0]) for s in segments]
    got = {k: shifted(b, sign * k) for k, b in base.items()}
    index = find_index(got[next(iter(more))])[0, 0]
    for bit, k in enumerate(more):
        wanted = lax.bitwise_and(lax.shift_right_logical(index, bit), 1) > 0
        more[k] = lax.cond(wanted, lambda b, k=k: shifted(b, sign * k), lambda b: b, more[k])
    return [got[s[0]] if s[1] == 0 else more[s[0]] for s in segments]


def per_device(queries, documents, positives, inner_owner, inner_row, outer_owner, outer_row):
    rows, width = queries.shape
    dp, grp = lax.axis_size("dp"), lax.axis_size("grp")
    cap = -(-max(2, 2 * rows // (grp - 1)) // 4) * 4
    base = -(-2 * cap // 24) * 8
    shape = jax.ShapeDtypeStruct
    shifts = sorted(range(1, grp), key=lambda k: (abs(2 * k - grp), k))
    split_shifts = [k for k in shifts if 1 < k < grp - 1] if 4 < grp <= 8 else []
    if split_shifts:
        rest = [(k, base, cap - base) for k in split_shifts] + [(k, 0, cap) for k in shifts if k not in split_shifts]
        groups = [(1, [(k, 0, base) for k in split_shifts]), (2, rest)]
    else:
        groups = [(1, [(k, 0, -(-cap // 8) * 8) for k in shifts])]
    segments = [segment for _, members in groups for segment in members]
    inner_owner, inner_row = inner_owner.reshape(dp, rows), inner_row.reshape(dp, rows)
    outer_owner, outer_row = outer_owner.reshape(grp, rows), outer_row.reshape(grp, rows)
    far_blocks = [shape((s[2] * split, width // split), bf16) for split, members in groups for s in members]
    totals = [sum(s[2] * split for s in members) for split, members in groups]
    far_flops, near_flops = 2 * sum(totals) * rows * width, 2 * dp * rows * rows * width

    send = call(
        functools.partial(send_kernel, groups),
        far_blocks,
        outer_owner, outer_row, documents,
        scratch=[
            pltpu.VMEM((grp, rows), i32),
            pltpu.VMEM((grp, rows), i32),
            pltpu.VMEM((grp, rows), i32),
            pltpu.VMEM((rows, width), bf16),
            pltpu.SemaphoreType.DMA((3,)),
        ],
        flops=far_flops,
        in_space=ANY,
    )
    smem = pl.BlockSpec(memory_space=pltpu.SMEM)
    index = []

    def find_index(arrived):
        index.append(
            call(
                functools.partial(subset_kernel, split_shifts, base),
                shape((1, 1), i32),
                outer_owner, arrived,
                in_space=[VMEM, ANY],
                out_space=smem,
            )
        )
        return index[0]

    def same_index(arrived):
        return call(
            later_kernel, shape((1, 1), i32), index[0], arrived, query_grads,
            in_space=[smem, ANY, ANY],
            out_space=smem,
        )

    got = exchange(send, segments, find_index, 1)
    docs = lax.all_gather(documents, "dp", axis=0, tiled=True)
    all_queries = lax.all_gather(queries, "dp", axis=0, tiled=True)
    scores, times = call(
        near_kernel,
        [shape((dp * rows, rows), f32)] * 2,
        queries, inner_owner, inner_row, docs,
        flops=near_flops,
    )
    far_weights = [shape((total, rows), bf16) for total in totals]
    far_stacks = [shape((total, width // split), bf16) for total, (split, _) in zip(totals, groups)]
    losses, near_w, *out = call(
        functools.partial(main_kernel, groups),
        [shape((1, rows), f32), shape((dp * rows, rows), bf16)] + far_blocks + far_weights + far_stacks,
        queries, scores, times, positives.reshape(1, rows), outer_owner, *got,
        flops=2 * far_flops,
    )
    far_grads, far = out[: len(segments)], out[len(segments) :]
    query_grads = call(
        functools.partial(query_grad_kernel, groups),
        shape((rows, width), bf16),
        near_w, docs, *far,
        flops=far_flops + near_flops,
    )
    back = exchange(far_grads, segments, same_index, -1)
    all_weights = lax.all_gather(near_w, "dp", axis=0, tiled=True)
    near_grads = call(near_grad_kernel, shape((rows, width), f32), all_weights, all_queries, flops=near_flops)
    doc_grads = call(
        functools.partial(far_grad_kernel, groups),
        shape((rows, width), bf16),
        near_grads, outer_owner, outer_row, *back,
        scratch=[pltpu.VMEM((grp, rows), i32)],
        flops=far_flops,
    )
    return losses.reshape(rows), query_grads, doc_grads


def solution(mesh):
    return jax.shard_map(
        per_device,
        mesh=mesh,
        in_specs=(
            P(("grp", "dp"), None),
            P(("grp", "dp"), None),
            P(("grp", "dp")),
            P("grp", None, None),
            P("grp", None, None),
            P("dp", None, None, None),
            P("dp", None, None, None),
        ),
        out_specs=(P(("grp", "dp")), P(("grp", "dp"), None), P(("grp", "dp"), None)),
        check_vma=False,
    )
```

```python
import functools

import jax
import jax.numpy as jnp
from jax import lax
from jax.experimental import pallas as pl
from jax.experimental.pallas import tpu as pltpu
from jax.sharding import PartitionSpec as P

COLUMNS = 4
SCALE = 3.0
VMEM = pl.BlockSpec(memory_space=pltpu.VMEM)
f32, bf16, i32 = jnp.float32, jnp.bfloat16, jnp.int32


ANY = pl.BlockSpec(memory_space=pl.ANY)


def call(kernel, out_shape, *args, scratch=(), flops=0, in_space=VMEM, out_space=VMEM, vmem=24):
    nbytes = sum(a.size * a.dtype.itemsize for a in (*args, *jax.tree.leaves(out_shape)))
    return pl.pallas_call(
        kernel,
        out_shape=out_shape,
        in_specs=in_space if isinstance(in_space, list) else [in_space] * len(args),
        out_specs=jax.tree.map(lambda _: out_space, out_shape),
        scratch_shapes=list(scratch),
        compiler_params=pltpu.CompilerParams(vmem_limit_bytes=vmem * 2**20),
        cost_estimate=pl.CostEstimate(flops=flops, bytes_accessed=nbytes, transcendentals=0),
    )(*args)


def dot(a, b, dims=((1,), (0,))):
    return lax.dot_general(a, b, (dims, ((), ())), preferred_element_type=f32)


NT = ((1,), (1,))
TN = ((0,), (0,))


def row_plan(segments, split):
    slots, chunks = [], []
    for _, first, count in segments:
        t = lax.broadcasted_iota(i32, (count * split, 128), 0)
        chunk = jnp.zeros_like(t)
        for c in range(1, split):
            chunk = chunk + (t >= c * count).astype(i32)
        slots.append(t - count * chunk + first)
        chunks.append(chunk)
    return jnp.concatenate(slots, axis=0), jnp.concatenate(chunks, axis=0)


def bounds(segments, split):
    ends = [0]
    for segment in segments:
        ends.append(ends[-1] + segment[2] * split)
    return list(zip(ends[:-1], ends[1:]))


def stacked(ref, split):
    width = ref.shape[1] // split
    return jnp.concatenate([ref[:, c * width : (c + 1) * width] for c in range(split)], axis=0)


def spread(values, chunk, split):
    if split == 1:
        return values.astype(bf16)
    return jnp.concatenate([jnp.where(chunk == c, values, 0.0).astype(bf16) for c in range(split)], axis=1)


def slot_codes(owner_ref, codes):
    peers, rows = owner_ref.shape
    me = lax.axis_index("grp")
    name = lax.rem(me - lax.broadcasted_iota(i32, (peers, rows), 0) - 1 + 2 * peers, peers)
    wanted = owner_ref[...] == name
    earlier = lax.broadcasted_iota(i32, (rows, rows), 0) < lax.broadcasted_iota(i32, (rows, rows), 1)
    rank = dot(wanted.astype(f32).astype(bf16), earlier.astype(f32).astype(bf16))
    codes[...] = jnp.where(wanted, rank, -1.0).astype(i32)


def slot_onehot(codes, row_ref, segments, split):
    slot, chunk = row_plan(segments, split)
    asked = []
    for (shift, _, _), (start, end) in zip(segments, bounds(segments, split)):
        r = lax.rem(lax.axis_index("grp") + shift, codes.shape[0])
        chosen = codes[pl.ds(r, 1), :] == slot[start:end]
        asked.append(jnp.where(chosen, row_ref[pl.ds(r, 1), :] + 1, 0).astype(f32))
    at = jnp.sum(jnp.concatenate(asked, axis=0), axis=1, keepdims=True)
    ids = lax.broadcasted_iota(i32, slot.shape, 1) + 1
    return jnp.where(ids.astype(f32) == at, 1.0, 0.0), chunk


def pick(items, groups):
    items = iter(items)
    return [[next(items) for _ in segments] for _, segments in groups]


def send_kernel(groups, owner_hbm, row_hbm, docs_hbm, *refs):
    *outs, codes, owner_ref, row_ref, docs_ref, sems = refs
    copies = [
        pltpu.make_async_copy(src, dst, sems.at[n])
        for n, (src, dst) in enumerate(((owner_hbm, owner_ref), (row_hbm, row_ref), (docs_hbm, docs_ref)))
    ]
    for copy in copies:
        copy.start()
    for copy in copies:
        copy.wait()
    slot_codes(owner_ref, codes)
    for (split, segments), blocks in zip(groups, pick(outs, groups)):
        onehot, chunk = slot_onehot(codes, row_ref, segments, split)
        rows = dot(spread(onehot, chunk, split), stacked(docs_ref, split))
        for (start, end), out in zip(bounds(segments, split), blocks):
            out[...] = rows[start:end].astype(bf16)


def subset_kernel(shifts, base, owner_ref, _, out):
    index = jnp.int32(0)
    for n, shift in enumerate(shifts):
        hits = (owner_ref[...] == owner_ref.shape[0] - 1 - shift).astype(f32)
        most = jnp.max(jnp.sum(hits, axis=1, keepdims=True))
        index = index + jnp.where(most > base, 1 << n, 0).astype(i32)
    out[0, 0] = index


def later_kernel(index_ref, *refs):
    refs[-1][0, 0] = index_ref[0, 0]


def live_count(owner_ref, shift):
    hit = owner_ref[pl.ds(lax.axis_index("grp"), 1), :] == owner_ref.shape[0] - 1 - shift
    return jnp.sum(hit.astype(f32), axis=1, keepdims=True).astype(i32)


def near_kernel(q_ref, owner_ref, row_ref, docs_ref, scores_out, times_out):
    me = lax.axis_index("dp")
    rows = q_ref.shape[0]
    owner, row = owner_ref[pl.ds(me, 1), :], row_ref[pl.ds(me, 1), :]
    same_row = row == lax.broadcasted_iota(i32, (rows, rows), 0)
    for d in range(owner_ref.shape[0]):
        part = slice(d * rows, (d + 1) * rows)
        times = jnp.sum((same_row & (owner == d)).astype(f32), axis=1, keepdims=True)
        times = jnp.broadcast_to(times + jnp.where(me == d, 1.0, 0.0), (rows, rows))
        scores = SCALE * dot(docs_ref[part, :], q_ref[...], NT)
        times_out[part, :] = times
        scores_out[part, :] = jnp.where(times > 0.0, scores, -jnp.inf)


def main_kernel(groups, q_ref, near_ref, times_ref, pos_ref, owner_ref, *refs):
    nseg = sum(len(segments) for _, segments in groups)
    blocks, refs = pick(refs[:nseg], groups), refs[nseg:]
    loss_out, near_w, *refs = refs
    dp = near_ref.shape[0] // q_ref.shape[0]
    peer_ws, refs = refs[:dp], refs[dp:]
    grads, refs = pick(refs[:nseg], groups), refs[nseg:]
    far_ws, fars = refs[: len(groups)], refs[len(groups) :]
    near = near_ref[...]
    top = jnp.max(near, axis=0, keepdims=True)
    all_scores = []
    for (split, segments), received, far in zip(groups, blocks, fars):
        slot, chunk = row_plan(segments, split)
        far[...] = jnp.concatenate([block[...] for block in received], axis=0)
        width = far.shape[1]
        part = dot(far[...], q_ref[:, :width], NT)
        for c in range(1, split):
            part = jnp.where(chunk == c, dot(far[...], q_ref[:, c * width : (c + 1) * width], NT), part)
        scores = []
        for segment, (start, end) in zip(segments, bounds(segments, split)):
            total = part[start:end]
            for c in range(1, split):
                total = total + pltpu.roll(part[start:end], c * segment[2], 0)
            live = live_count(owner_ref, segment[0])
            scores.append(jnp.where(slot[start:end] < live, SCALE * total, -jnp.inf))
        scores = jnp.concatenate(scores, axis=0)
        all_scores.append(scores)
        top = jnp.maximum(top, jnp.max(scores, axis=0, keepdims=True))
    near_e = times_ref[...] * jnp.exp(near - top)
    total = jnp.sum(near_e, axis=0, keepdims=True)
    all_e = []
    for (split, segments), scores in zip(groups, all_scores):
        _, chunk = row_plan(segments, split)
        e = jnp.exp(scores - top)
        all_e.append(e)
        total = total + jnp.sum(jnp.where(chunk == 0, e, 0.0), axis=0, keepdims=True)
    factor = SCALE / total
    for (split, segments), e, outs, far_w in zip(groups, all_e, grads, far_ws):
        _, chunk = row_plan(segments, split)
        w = e * factor
        far_w[...] = w.astype(bf16)
        rows = dot(spread(w, chunk, split), stacked(q_ref, split))
        for (start, end), out in zip(bounds(segments, split), outs):
            out[...] = rows[start:end].astype(bf16)
    rows = q_ref.shape[0]
    own = lax.axis_index("dp") * rows
    positive = (lax.broadcasted_iota(i32, near.shape, 0) == pos_ref[...] + own).astype(f32)
    loss_out[...] = top + jnp.log(total) - jnp.sum(jnp.where(positive > 0.0, near, 0.0), axis=0, keepdims=True)
    near_w[...] = (near_e * factor - SCALE * positive).astype(bf16)
    for shift, out in enumerate(peer_ws):
        peer = lax.rem(lax.axis_index("dp") + shift, dp)
        out[...] = near_w[pl.ds(pl.multiple_of(peer * rows, rows), rows), :]


def add_groups(groups, selects, blocks, acc, cols):
    for (split, segments), select, block in zip(groups, selects, blocks):
        width = block.shape[1]
        chunk = cols.start // width
        if split > 1:
            select = jnp.where(row_plan(segments, split)[1] == chunk, select, 0.0)
        acc = acc + dot(select.astype(bf16), block[:, cols.start - chunk * width : cols.stop - chunk * width], TN)
    return acc


def query_grad_kernel(groups, near_w, docs_ref, *refs):
    *refs, out = refs
    refs = refs[: 2 * len(groups)]
    selects, blocks = [ref[...].astype(f32) for ref in refs[: len(groups)]], refs[len(groups) :]
    width = out.shape[1] // COLUMNS
    for c in range(COLUMNS):
        cols = slice(c * width, (c + 1) * width)
        acc = dot(near_w[...], docs_ref[:, cols], TN)
        out[:, cols] = add_groups(groups, selects, blocks, acc, cols).astype(bf16)


def near_grad_kernel(q_ref, *refs):
    *weights, out = refs
    rows, peers = out.shape[0], len(weights)
    acc = jnp.zeros(out.shape, f32)
    for shift, w in enumerate(weights):
        peer = lax.rem(lax.axis_index("dp") - shift + peers, peers)
        acc = acc + dot(w[...], q_ref[pl.ds(pl.multiple_of(peer * rows, rows), rows), :])
    out[...] = acc


def far_grad_kernel(groups, near_ref, owner_ref, row_ref, *refs):
    *refs, out, codes = refs
    slot_codes(owner_ref, codes)
    selects = [slot_onehot(codes, row_ref, segments, split)[0] for split, segments in groups]
    blocks = [jnp.concatenate([block[...] for block in received], axis=0) for received in pick(refs, groups)]
    width = out.shape[1] // COLUMNS
    for c in range(COLUMNS):
        cols = slice(c * width, (c + 1) * width)
        out[:, cols] = add_groups(groups, selects, blocks, near_ref[:, cols], cols).astype(bf16)


def shifted(block, shift, axis="grp"):
    size = lax.axis_size(axis)
    return lax.ppermute(block, axis, [(g, (g + shift) % size) for g in range(size)])


def exchange(blocks, segments, find_index, sign):
    base = {s[0]: b for s, b in zip(segments, blocks) if s[1] == 0}
    more = {s[0]: b for s, b in zip(segments, blocks) if s[1] > 0}
    if not more:
        return [shifted(base[s[0]], sign * s[0]) for s in segments]
    got = {k: shifted(b, sign * k) for k, b in base.items()}
    index = find_index(got[next(iter(more))])[0, 0]
    for bit, k in enumerate(more):
        wanted = lax.bitwise_and(lax.shift_right_logical(index, bit), 1) > 0
        more[k] = lax.cond(wanted, lambda b, k=k: shifted(b, sign * k), lambda b: b, more[k])
    return [got[s[0]] if s[1] == 0 else more[s[0]] for s in segments]


def per_device(queries, documents, positives, inner_owner, inner_row, outer_owner, outer_row):
    rows, width = queries.shape
    dp, grp = lax.axis_size("dp"), lax.axis_size("grp")
    cap = -(-max(2, 2 * rows // (grp - 1)) // 4) * 4
    base = -(-2 * cap // 24) * 8
    shape = jax.ShapeDtypeStruct
    shifts = sorted(range(1, grp), key=lambda k: (abs(2 * k - grp), k))
    split_shifts = [k for k in shifts if 1 < k < grp - 1] if False else []
    if split_shifts:
        rest = [(k, base, cap - base) for k in split_shifts] + [(k, 0, cap) for k in shifts if k not in split_shifts]
        groups = [(1, [(k, 0, base) for k in split_shifts]), (2, rest)]
    else:
        groups = [(2, [(k, 0, cap) for k in shifts])]
    segments = [segment for _, members in groups for segment in members]
    inner_owner, inner_row = inner_owner.reshape(dp, rows), inner_row.reshape(dp, rows)
    outer_owner, outer_row = outer_owner.reshape(grp, rows), outer_row.reshape(grp, rows)
    far_blocks = [shape((s[2] * split, width // split), bf16) for split, members in groups for s in members]
    totals = [sum(s[2] * split for s in members) for split, members in groups]
    far_flops, near_flops = 2 * sum(totals) * rows * width, 2 * dp * rows * rows * width

    send = call(
        functools.partial(send_kernel, groups),
        far_blocks,
        outer_owner, outer_row, documents,
        scratch=[
            pltpu.VMEM((grp, rows), i32),
            pltpu.VMEM((grp, rows), i32),
            pltpu.VMEM((grp, rows), i32),
            pltpu.VMEM((rows, width), bf16),
            pltpu.SemaphoreType.DMA((3,)),
        ],
        flops=far_flops,
        in_space=ANY,
    )
    smem = pl.BlockSpec(memory_space=pltpu.SMEM)
    index = []

    def find_index(arrived):
        index.append(
            call(
                functools.partial(subset_kernel, split_shifts, base),
                shape((1, 1), i32),
                outer_owner, arrived,
                in_space=[VMEM, ANY],
                out_space=smem,
            )
        )
        return index[0]

    def same_index(arrived):
        return call(
            later_kernel, shape((1, 1), i32), index[0], arrived, query_grads,
            in_space=[smem, ANY, ANY],
            out_space=smem,
        )

    got = exchange(send, segments, find_index, 1)
    docs = lax.all_gather(documents, "dp", axis=0, tiled=True)
    all_queries = lax.all_gather(queries, "dp", axis=0, tiled=True)
    scores, times = call(
        near_kernel,
        [shape((dp * rows, rows), f32)] * 2,
        queries, inner_owner, inner_row, docs,
        flops=near_flops,
    )
    far_weights = [shape((total, rows), bf16) for total in totals]
    far_stacks = [shape((total, width // split), bf16) for total, (split, _) in zip(totals, groups)]
    weight = shape((rows, rows), bf16)
    losses, near_w, *out = call(
        functools.partial(main_kernel, groups),
        [shape((1, rows), f32), shape((dp * rows, rows), bf16)] + [weight] * dp + far_blocks + far_weights + far_stacks,
        queries, scores, times, positives.reshape(1, rows), outer_owner, *got,
        flops=2 * far_flops,
    )
    peer_w, far_grads, far = out[:dp], out[dp : dp + len(segments)], out[dp + len(segments) :]
    peer_w = [shifted(w, n, "dp") if n else w for n, w in enumerate(peer_w)]
    query_grads = call(
        functools.partial(query_grad_kernel, groups),
        shape((rows, width), bf16),
        near_w, docs, *far, *peer_w[1:],
        flops=far_flops + near_flops,
        in_space=[VMEM] * (2 + len(far)) + [ANY] * (dp - 1),
    )
    back = exchange(far_grads, segments, same_index, -1)
    near_grads = call(near_grad_kernel, shape((rows, width), f32), all_queries, *peer_w, flops=near_flops)
    doc_grads = call(
        functools.partial(far_grad_kernel, groups),
        shape((rows, width), bf16),
        near_grads, outer_owner, outer_row, *back,
        scratch=[pltpu.VMEM((grp, rows), i32)],
        flops=far_flops,
    )
    return losses.reshape(rows), query_grads, doc_grads


def solution(mesh):
    return jax.shard_map(
        per_device,
        mesh=mesh,
        in_specs=(
            P(("grp", "dp"), None),
            P(("grp", "dp"), None),
            P(("grp", "dp")),
            P("grp", None, None),
            P("grp", None, None),
            P("dp", None, None, None),
            P("dp", None, None, None),
        ),
        out_specs=(P(("grp", "dp")), P(("grp", "dp"), None), P(("grp", "dp"), None)),
        check_vma=False,
    )
```

```python
import functools
from typing import NamedTuple

import jax
import jax.numpy as jnp
from jax import lax
from jax.experimental import pallas as pl
from jax.experimental.pallas import tpu as pltpu
from jax.sharding import PartitionSpec as P

COLUMNS = 4
SCALE = 3.0
VMEM = pl.BlockSpec(memory_space=pltpu.VMEM)
ANY = pl.BlockSpec(memory_space=pl.ANY)
f32, bf16, i32 = jnp.float32, jnp.bfloat16, jnp.int32


class Blocks(NamedTuple):
    axis: str
    shifts: tuple
    count: int
    split: int

    @property
    def rows(self):
        return self.count * self.split

    @property
    def total(self):
        return self.rows * len(self.shifts)

    def part(self, n):
        return slice(n * self.rows, (n + 1) * self.rows)


def call(kernel, out_shape, *args, scratch=(), flops=0, unread=0, vmem=24):
    nbytes = sum(a.size * a.dtype.itemsize for a in (*args, *jax.tree.leaves(out_shape)))
    read = len(args) - unread

    def body(*refs):
        kernel(*refs[:read], *refs[len(args) :])

    return pl.pallas_call(
        body,
        out_shape=out_shape,
        in_specs=[VMEM] * read + [ANY] * unread,
        out_specs=jax.tree.map(lambda _: VMEM, out_shape),
        scratch_shapes=list(scratch),
        compiler_params=pltpu.CompilerParams(vmem_limit_bytes=vmem * 2**20),
        cost_estimate=pl.CostEstimate(flops=flops, bytes_accessed=nbytes, transcendentals=0),
    )(*args)


def dot(a, b, dims=((1,), (0,))):
    return lax.dot_general(a, b, (dims, ((), ())), preferred_element_type=f32)


NT = ((1,), (1,))
TN = ((0,), (0,))


def row_plan(plan):
    t = lax.broadcasted_iota(i32, (plan.rows, 128), 0)
    chunk = jnp.zeros_like(t)
    for c in range(1, plan.split):
        chunk = chunk + (t >= c * plan.count).astype(i32)
    slot = t - plan.count * chunk
    return jnp.concatenate([slot] * len(plan.shifts), axis=0), jnp.concatenate([chunk] * len(plan.shifts), axis=0)


def stacked(ref, split):
    width = ref.shape[1] // split
    return jnp.concatenate([ref[:, c * width : (c + 1) * width] for c in range(split)], axis=0)


def spread(values, chunk, split):
    if split == 1:
        return values.astype(bf16)
    return jnp.concatenate([jnp.where(chunk == c, values, 0.0).astype(bf16) for c in range(split)], axis=1)


def slot_codes(axis, owner_ref, codes):
    peers, rows = owner_ref.shape
    name = me = lax.axis_index(axis)
    if axis == "grp":
        name = lax.rem(me - lax.broadcasted_iota(i32, (peers, rows), 0) - 1 + 2 * peers, peers)
    wanted = owner_ref[...] == name
    earlier = lax.broadcasted_iota(i32, (rows, rows), 0) < lax.broadcasted_iota(i32, (rows, rows), 1)
    rank = dot(wanted.astype(f32).astype(bf16), earlier.astype(f32).astype(bf16))
    codes[...] = jnp.where(wanted, rank, -1.0).astype(i32)


def slot_onehot(plan, codes, row_ref):
    slot, chunk = row_plan(plan)
    asked = []
    for n, shift in enumerate(plan.shifts):
        r = lax.rem(lax.axis_index(plan.axis) + shift, codes.shape[0])
        chosen = codes[pl.ds(r, 1), :] == slot[plan.part(n)]
        asked.append(jnp.where(chosen, row_ref[pl.ds(r, 1), :] + 1, 0).astype(f32))
    at = jnp.sum(jnp.concatenate(asked, axis=0), axis=1, keepdims=True)
    ids = lax.broadcasted_iota(i32, slot.shape, 1) + 1
    return jnp.where(ids.astype(f32) == at, 1.0, 0.0), chunk


def live_slots(plan, owner_ref):
    slot, _ = row_plan(plan)
    peers = owner_ref.shape[0]
    me = lax.axis_index(plan.axis)
    live = []
    for n, shift in enumerate(plan.shifts):
        name = peers - 1 - shift if plan.axis == "grp" else lax.rem(me - shift + peers, peers)
        used = jnp.sum((owner_ref[pl.ds(me, 1), :] == name).astype(f32), axis=1, keepdims=True)
        live.append(slot[plan.part(n)].astype(f32) < used)
    return jnp.concatenate(live, axis=0)


def send_kernel(plan, owner_ref, row_ref, docs_ref, *refs):
    *outs, codes = refs
    slot_codes(plan.axis, owner_ref, codes)
    onehot, chunk = slot_onehot(plan, codes, row_ref)
    rows = dot(spread(onehot, chunk, plan.split), stacked(docs_ref, plan.split))
    for n, out in enumerate(outs):
        out[...] = rows[plan.part(n)].astype(bf16)


def near_kernel(plan, q_ref, docs_ref, owner_ref, row_ref, *refs):
    *blocks, scores_out, times_out, inner_out = refs
    me = lax.axis_index("dp")
    rows = q_ref.shape[0]
    named = (owner_ref[pl.ds(me, 1), :] == me) & (row_ref[pl.ds(me, 1), :] == lax.broadcasted_iota(i32, (rows, rows), 0))
    times = 1.0 + jnp.sum(named.astype(f32), axis=1, keepdims=True)
    times_out[:rows, :] = jnp.broadcast_to(times, (rows, rows))
    times_out[rows:, :] = jnp.ones((plan.total, rows), f32)
    scores_out[:rows, :] = SCALE * dot(docs_ref[...], q_ref[...], NT)
    inner_out[...] = jnp.concatenate([block[...] for block in blocks], axis=0)
    scores = SCALE * dot(inner_out[...], q_ref[...], NT)
    scores_out[rows:, :] = jnp.where(live_slots(plan, owner_ref), scores, -jnp.inf)


def main_kernel(plan, q_ref, near_ref, times_ref, pos_ref, owner_ref, *refs):
    blocks, refs = refs[: len(plan.shifts)], refs[len(plan.shifts) :]
    loss_out, near_w, far_w, far, *grads = refs
    rows = q_ref.shape[0]
    _, chunk = row_plan(plan)
    far[...] = jnp.concatenate([block[...] for block in blocks], axis=0)
    width = far.shape[1]
    part = dot(far[...], q_ref[:, :width], NT)
    for c in range(1, plan.split):
        part = jnp.where(chunk == c, dot(far[...], q_ref[:, c * width : (c + 1) * width], NT), part)
    scores = []
    for n in range(len(blocks)):
        total = part[plan.part(n)]
        for c in range(1, plan.split):
            total = total + pltpu.roll(part[plan.part(n)], c * plan.count, 0)
        scores.append(total)
    scores = jnp.where(live_slots(plan, owner_ref), SCALE * jnp.concatenate(scores, axis=0), -jnp.inf)
    near = near_ref[...]
    top = jnp.maximum(jnp.max(near, axis=0, keepdims=True), jnp.max(scores, axis=0, keepdims=True))
    near_e = times_ref[...] * jnp.exp(near - top)
    far_e = jnp.exp(scores - top)
    total = jnp.sum(near_e, axis=0, keepdims=True)
    total = total + jnp.sum(jnp.where(chunk == 0, far_e, 0.0), axis=0, keepdims=True)
    factor = SCALE / total
    w = far_e * factor
    far_w[...] = w.astype(bf16)
    sums = dot(spread(w, chunk, plan.split), stacked(q_ref, plan.split))
    for n, out in enumerate(grads):
        out[...] = sums[plan.part(n)].astype(bf16)
    positive = (lax.broadcasted_iota(i32, near.shape, 0) == pos_ref[...]).astype(f32)
    loss_out[...] = top + jnp.log(total) - jnp.sum(jnp.where(positive > 0.0, near, 0.0), axis=0, keepdims=True)
    near_w[...] = (near_e * factor - SCALE * positive).astype(bf16)


def inner_grad_kernel(plan, near_w, q_ref, *outs):
    sums = dot(near_w[q_ref.shape[0] :, :], q_ref[...])
    for n, out in enumerate(outs):
        out[...] = sums[plan.part(n)].astype(bf16)


def add_far(plan, select, block, acc, cols):
    width = block.shape[1]
    chunk = cols.start // width
    if plan.split > 1:
        select = jnp.where(row_plan(plan)[1] == chunk, select, 0.0)
    return acc + dot(select.astype(bf16), block[:, cols.start - chunk * width : cols.stop - chunk * width], TN)


def query_grad_kernel(plan, near_w, docs_ref, inner_ref, far_w, far_ref, out):
    rows = docs_ref.shape[0]
    width = out.shape[1] // COLUMNS
    far_w = far_w[...].astype(f32)
    for c in range(COLUMNS):
        cols = slice(c * width, (c + 1) * width)
        acc = dot(near_w[:rows, :], docs_ref[:, cols], TN) + dot(near_w[rows:, :], inner_ref[:, cols], TN)
        out[:, cols] = add_far(plan, far_w, far_ref, acc, cols).astype(bf16)


def near_grad_kernel(plan, near_w, q_ref, owner_ref, row_ref, *refs):
    *blocks, out, codes = refs
    slot_codes(plan.axis, owner_ref, codes)
    onehot, _ = slot_onehot(plan, codes, row_ref)
    block = jnp.concatenate([block[...] for block in blocks], axis=0)
    out[...] = dot(near_w[: q_ref.shape[0], :], q_ref[...]) + dot(onehot.astype(bf16), block, TN)


def doc_grad_kernel(plan, near_ref, owner_ref, row_ref, *refs):
    *blocks, out, codes = refs
    slot_codes(plan.axis, owner_ref, codes)
    onehot, _ = slot_onehot(plan, codes, row_ref)
    block = jnp.concatenate([block[...] for block in blocks], axis=0)
    width = out.shape[1] // COLUMNS
    for c in range(COLUMNS):
        cols = slice(c * width, (c + 1) * width)
        out[:, cols] = add_far(plan, onehot, block, near_ref[:, cols], cols).astype(bf16)


def exchange(plan, blocks, sign):
    size = lax.axis_size(plan.axis)
    return [
        lax.ppermute(block, plan.axis, [(g, (g + sign * shift) % size) for g in range(size)])
        for shift, block in zip(plan.shifts, blocks)
    ]


def per_device(queries, documents, positives, inner_owner, inner_row, outer_owner, outer_row):
    rows, width = queries.shape
    dp, grp = lax.axis_size("dp"), lax.axis_size("grp")
    cap_inner = -(-max(2, 2 * rows // dp) // 16) * 16
    cap_outer = -(-max(2, 2 * rows // (grp - 1)) // 4) * 4
    inner = Blocks("dp", tuple(range(1, dp)), cap_inner, 1)
    outer_shifts = tuple(sorted(range(1, grp), key=lambda k: (abs(2 * k - grp), k)))
    outer = Blocks("grp", outer_shifts, cap_outer, 1 if cap_outer % 8 == 0 else 2)
    inner_owner, inner_row = inner_owner.reshape(dp, rows), inner_row.reshape(dp, rows)
    outer_owner, outer_row = outer_owner.reshape(grp, rows), outer_row.reshape(grp, rows)
    shape = jax.ShapeDtypeStruct
    outer_blocks = [shape((outer.rows, width // outer.split), bf16)] * len(outer.shifts)
    inner_blocks = [shape((inner.rows, width), bf16)] * len(inner.shifts)
    outer_codes, inner_codes = [pltpu.VMEM((grp, rows), i32)], [pltpu.VMEM((dp, rows), i32)]
    far_flops, inner_flops, own_flops = 2 * outer.total * rows * width, 2 * inner.total * rows * width, 2 * rows * rows * width

    send = call(
        functools.partial(send_kernel, outer),
        outer_blocks,
        outer_owner, outer_row, documents,
        scratch=outer_codes, flops=far_flops,
    )
    got = exchange(outer, send, 1)
    send_inner = call(
        functools.partial(send_kernel, inner),
        inner_blocks,
        inner_owner, inner_row, documents,
        scratch=inner_codes, flops=inner_flops, unread=0,
    )
    got_inner = exchange(inner, send_inner, 1)
    scores, times, inner_rows = call(
        functools.partial(near_kernel, inner),
        [shape((rows + inner.total, rows), f32)] * 2 + [shape((inner.total, width), bf16)],
        queries, documents, inner_owner, inner_row, *got_inner, got[0], got[1], got[2],
        flops=inner_flops + own_flops, unread=3,
    )
    losses, near_w, far_w, far_rows, *grads = call(
        functools.partial(main_kernel, outer),
        [
            shape((1, rows), f32),
            shape((rows + inner.total, rows), bf16),
            shape((outer.total, rows), bf16),
            shape((outer.total, width // outer.split), bf16),
            *outer_blocks,
        ],
        queries, scores, times, positives.reshape(1, rows), outer_owner, *got,
        flops=2 * far_flops,
    )
    back = exchange(outer, grads, -1)
    query_grads = call(
        functools.partial(query_grad_kernel, outer),
        shape((rows, width), bf16),
        near_w, documents, inner_rows, far_w, far_rows,
        flops=far_flops + inner_flops + own_flops,
    )
    grads_inner = call(
        functools.partial(inner_grad_kernel, inner),
        inner_blocks,
        near_w, queries,
        flops=inner_flops, unread=0,
    )
    back_inner = exchange(inner, grads_inner, -1)
    near_grads = call(
        functools.partial(near_grad_kernel, inner),
        shape((rows, width), f32),
        near_w, queries, inner_owner, inner_row, *back_inner, back[0], back[1], back[2],
        scratch=inner_codes, flops=inner_flops + own_flops, unread=3,
    )
    doc_grads = call(
        functools.partial(doc_grad_kernel, outer),
        shape((rows, width), bf16),
        near_grads, outer_owner, outer_row, *back,
        scratch=outer_codes, flops=far_flops,
    )
    return losses.reshape(rows), query_grads, doc_grads


def solution(mesh):
    return jax.shard_map(
        per_device,
        mesh=mesh,
        in_specs=(
            P(("grp", "dp"), None),
            P(("grp", "dp"), None),
            P(("grp", "dp")),
            P("grp", None, None),
            P("grp", None, None),
            P("dp", None, None, None),
            P("dp", None, None, None),
        ),
        out_specs=(P(("grp", "dp")), P(("grp", "dp"), None), P(("grp", "dp"), None)),
        check_vma=False,
    )
```

```python
import functools
from typing import NamedTuple

import jax
import jax.numpy as jnp
from jax import lax
from jax.experimental import pallas as pl
from jax.experimental.pallas import tpu as pltpu
from jax.sharding import PartitionSpec as P

COLUMNS = 4
OUTER_ORDER = {8: (4, 5, 3, 2, 7, 6, 1)}
INNER_ORDER = {4: (3, 2, 1)}
SCALE = 3.0
VMEM = pl.BlockSpec(memory_space=pltpu.VMEM)
ANY = pl.BlockSpec(memory_space=pl.ANY)
f32, bf16, i32 = jnp.float32, jnp.bfloat16, jnp.int32


def peer_at(axis, shift, sign, size, me=None):
    me = lax.axis_index(axis) if me is None else me
    return lax.rem(me + sign * shift + size, size) if axis == "grp" else lax.bitwise_xor(me, jnp.int32(shift))


class Blocks(NamedTuple):
    axis: str
    shifts: tuple
    count: int
    split: int

    @property
    def rows(self):
        return self.count * self.split

    @property
    def total(self):
        return self.rows * len(self.shifts)

    def part(self, n):
        return slice(n * self.rows, (n + 1) * self.rows)


def call(kernel, out_shape, *args, scratch=(), flops=0, unread=0, vmem=24):
    nbytes = sum(a.size * a.dtype.itemsize for a in (*args, *jax.tree.leaves(out_shape)))
    read = len(args) - unread

    def body(*refs):
        kernel(*refs[:read], *refs[len(args) :])

    return pl.pallas_call(
        body,
        out_shape=out_shape,
        in_specs=[VMEM] * read + [ANY] * unread,
        out_specs=jax.tree.map(lambda _: VMEM, out_shape),
        scratch_shapes=list(scratch),
        compiler_params=pltpu.CompilerParams(vmem_limit_bytes=vmem * 2**20),
        cost_estimate=pl.CostEstimate(flops=flops, bytes_accessed=nbytes, transcendentals=0),
    )(*args)


def dot(a, b, dims=((1,), (0,))):
    return lax.dot_general(a, b, (dims, ((), ())), preferred_element_type=f32)


NT = ((1,), (1,))
TN = ((0,), (0,))


def row_plan(plan):
    t = lax.broadcasted_iota(i32, (plan.rows, 128), 0)
    chunk = jnp.zeros_like(t)
    for c in range(1, plan.split):
        chunk = chunk + (t >= c * plan.count).astype(i32)
    slot = t - plan.count * chunk
    return jnp.concatenate([slot] * len(plan.shifts), axis=0), jnp.concatenate([chunk] * len(plan.shifts), axis=0)


def stacked(ref, split):
    width = ref.shape[1] // split
    return jnp.concatenate([ref[:, c * width : (c + 1) * width] for c in range(split)], axis=0)


def spread(values, chunk, split):
    if split == 1:
        return values.astype(bf16)
    return jnp.concatenate([jnp.where(chunk == c, values, 0.0).astype(bf16) for c in range(split)], axis=1)


def slot_codes(axis, owner_ref, codes):
    peers, rows = owner_ref.shape
    name = me = lax.axis_index(axis)
    if axis == "grp":
        name = lax.rem(me - lax.broadcasted_iota(i32, (peers, rows), 0) - 1 + 2 * peers, peers)
    wanted = owner_ref[...] == name
    earlier = lax.broadcasted_iota(i32, (rows, rows), 0) < lax.broadcasted_iota(i32, (rows, rows), 1)
    rank = dot(wanted.astype(f32).astype(bf16), earlier.astype(f32).astype(bf16))
    codes[...] = jnp.where(wanted, rank, -1.0).astype(i32)


def slot_onehot(plan, codes, row_ref):
    slot, chunk = row_plan(plan)
    asked = []
    for n, shift in enumerate(plan.shifts):
        r = peer_at(plan.axis, shift, 1, codes.shape[0])
        chosen = codes[pl.ds(r, 1), :] == slot[plan.part(n)]
        asked.append(jnp.where(chosen, row_ref[pl.ds(r, 1), :] + 1, 0).astype(f32))
    at = jnp.sum(jnp.concatenate(asked, axis=0), axis=1, keepdims=True)
    ids = lax.broadcasted_iota(i32, slot.shape, 1) + 1
    return jnp.where(ids.astype(f32) == at, 1.0, 0.0), chunk


def live_slots(plan, owner_ref):
    slot, _ = row_plan(plan)
    peers = owner_ref.shape[0]
    me = lax.axis_index(plan.axis)
    live = []
    for n, shift in enumerate(plan.shifts):
        name = peers - 1 - shift if plan.axis == "grp" else peer_at("dp", shift, -1, peers)
        used = jnp.sum((owner_ref[pl.ds(me, 1), :] == name).astype(f32), axis=1, keepdims=True)
        live.append(slot[plan.part(n)].astype(f32) < used)
    return jnp.concatenate(live, axis=0)


def send_kernel(plan, owner_ref, row_ref, docs_ref, *refs):
    *outs, codes = refs
    slot_codes(plan.axis, owner_ref, codes)
    onehot, chunk = slot_onehot(plan, codes, row_ref)
    rows = dot(spread(onehot, chunk, plan.split), stacked(docs_ref, plan.split))
    for n, out in enumerate(outs):
        out[...] = rows[plan.part(n)].astype(bf16)


def near_kernel(plan, q_ref, docs_ref, owner_ref, row_ref, *refs):
    *blocks, scores_out, times_out, inner_out = refs
    me = lax.axis_index("dp")
    rows = q_ref.shape[0]
    named = (owner_ref[pl.ds(me, 1), :] == me) & (row_ref[pl.ds(me, 1), :] == lax.broadcasted_iota(i32, (rows, rows), 0))
    times = 1.0 + jnp.sum(named.astype(f32), axis=1, keepdims=True)
    times_out[:rows, :] = jnp.broadcast_to(times, (rows, rows))
    times_out[rows:, :] = jnp.ones((plan.total, rows), f32)
    scores_out[:rows, :] = SCALE * dot(docs_ref[...], q_ref[...], NT)
    inner_out[...] = jnp.concatenate([block[...] for block in blocks], axis=0)
    scores = SCALE * dot(inner_out[...], q_ref[...], NT)
    scores_out[rows:, :] = jnp.where(live_slots(plan, owner_ref), scores, -jnp.inf)


def main_kernel(plan, q_ref, near_ref, times_ref, pos_ref, owner_ref, *refs):
    blocks, refs = refs[: len(plan.shifts)], refs[len(plan.shifts) :]
    loss_out, near_w, far_w, far, *grads = refs
    rows = q_ref.shape[0]
    _, chunk = row_plan(plan)
    far[...] = jnp.concatenate([block[...] for block in blocks], axis=0)
    width = far.shape[1]
    part = dot(far[...], q_ref[:, :width], NT)
    for c in range(1, plan.split):
        part = jnp.where(chunk == c, dot(far[...], q_ref[:, c * width : (c + 1) * width], NT), part)
    scores = []
    for n in range(len(blocks)):
        total = part[plan.part(n)]
        for c in range(1, plan.split):
            total = total + pltpu.roll(part[plan.part(n)], c * plan.count, 0)
        scores.append(total)
    scores = jnp.where(live_slots(plan, owner_ref), SCALE * jnp.concatenate(scores, axis=0), -jnp.inf)
    near = near_ref[...]
    top = jnp.maximum(jnp.max(near, axis=0, keepdims=True), jnp.max(scores, axis=0, keepdims=True))
    near_e = times_ref[...] * jnp.exp(near - top)
    far_e = jnp.exp(scores - top)
    total = jnp.sum(near_e, axis=0, keepdims=True)
    total = total + jnp.sum(jnp.where(chunk == 0, far_e, 0.0), axis=0, keepdims=True)
    factor = SCALE / total
    w = far_e * factor
    far_w[...] = w.astype(bf16)
    sums = dot(spread(w, chunk, plan.split), stacked(q_ref, plan.split))
    for n, out in enumerate(grads):
        out[...] = sums[plan.part(n)].astype(bf16)
    positive = (lax.broadcasted_iota(i32, near.shape, 0) == pos_ref[...]).astype(f32)
    loss_out[...] = top + jnp.log(total) - jnp.sum(jnp.where(positive > 0.0, near, 0.0), axis=0, keepdims=True)
    near_w[...] = (near_e * factor - SCALE * positive).astype(bf16)


def inner_grad_kernel(plan, near_w, q_ref, *outs):
    sums = dot(near_w[q_ref.shape[0] :, :], q_ref[...])
    for n, out in enumerate(outs):
        out[...] = sums[plan.part(n)].astype(bf16)


def add_far(plan, select, block, acc, cols):
    width = block.shape[1]
    chunk = cols.start // width
    if plan.split > 1:
        select = jnp.where(row_plan(plan)[1] == chunk, select, 0.0)
    return acc + dot(select.astype(bf16), block[:, cols.start - chunk * width : cols.stop - chunk * width], TN)


def query_grad_kernel(plan, near_w, docs_ref, inner_ref, far_w, far_ref, out):
    rows = docs_ref.shape[0]
    width = out.shape[1] // COLUMNS
    far_w = far_w[...].astype(f32)
    for c in range(COLUMNS):
        cols = slice(c * width, (c + 1) * width)
        acc = dot(near_w[:rows, :], docs_ref[:, cols], TN) + dot(near_w[rows:, :], inner_ref[:, cols], TN)
        out[:, cols] = add_far(plan, far_w, far_ref, acc, cols).astype(bf16)


def near_grad_kernel(plan, near_w, q_ref, owner_ref, row_ref, *refs):
    *blocks, out, codes = refs
    slot_codes(plan.axis, owner_ref, codes)
    onehot, _ = slot_onehot(plan, codes, row_ref)
    block = jnp.concatenate([block[...] for block in blocks], axis=0)
    out[...] = dot(near_w[: q_ref.shape[0], :], q_ref[...]) + dot(onehot.astype(bf16), block, TN)


def doc_grad_kernel(plan, near_ref, owner_ref, row_ref, *refs):
    *blocks, out, codes = refs
    slot_codes(plan.axis, owner_ref, codes)
    onehot, _ = slot_onehot(plan, codes, row_ref)
    block = jnp.concatenate([block[...] for block in blocks], axis=0)
    width = out.shape[1] // COLUMNS
    for c in range(COLUMNS):
        cols = slice(c * width, (c + 1) * width)
        out[:, cols] = add_far(plan, onehot, block, near_ref[:, cols], cols).astype(bf16)


def exchange(plan, blocks, sign):
    size = lax.axis_size(plan.axis)
    moved = []
    for shift, block in zip(plan.shifts, blocks):
        pairs = [(g, (g + sign * shift) % size if plan.axis == "grp" else g ^ shift) for g in range(size)]
        moved.append(lax.ppermute(block, plan.axis, pairs))
    return moved


def per_device(queries, documents, positives, inner_owner, inner_row, outer_owner, outer_row):
    rows, width = queries.shape
    dp, grp = lax.axis_size("dp"), lax.axis_size("grp")
    cap_inner = -(-max(2, 2 * rows // dp) // 16) * 16
    cap_outer = -(-max(2, 2 * rows // (grp - 1)) // 4) * 4
    inner = Blocks("dp", INNER_ORDER.get(dp, tuple(range(1, dp))), cap_inner, 1)
    outer_shifts = OUTER_ORDER.get(grp, tuple(range(1, grp)))
    outer = Blocks("grp", outer_shifts, cap_outer, 1 if cap_outer % 8 == 0 else 2)
    inner_owner, inner_row = inner_owner.reshape(dp, rows), inner_row.reshape(dp, rows)
    outer_owner, outer_row = outer_owner.reshape(grp, rows), outer_row.reshape(grp, rows)
    shape = jax.ShapeDtypeStruct
    outer_blocks = [shape((outer.rows, width // outer.split), bf16)] * len(outer.shifts)
    inner_blocks = [shape((inner.rows, width), bf16)] * len(inner.shifts)
    outer_codes, inner_codes = [pltpu.VMEM((grp, rows), i32)], [pltpu.VMEM((dp, rows), i32)]
    far_flops, inner_flops, own_flops = 2 * outer.total * rows * width, 2 * inner.total * rows * width, 2 * rows * rows * width

    send = call(
        functools.partial(send_kernel, outer),
        outer_blocks,
        outer_owner, outer_row, documents,
        scratch=outer_codes, flops=far_flops,
    )
    got = exchange(outer, send, 1)
    send_inner = call(
        functools.partial(send_kernel, inner),
        inner_blocks,
        inner_owner, inner_row, documents,
        scratch=inner_codes, flops=inner_flops, unread=0,
    )
    got_inner = exchange(inner, send_inner, 1)
    scores, times, inner_rows = call(
        functools.partial(near_kernel, inner),
        [shape((rows + inner.total, rows), f32)] * 2 + [shape((inner.total, width), bf16)],
        queries, documents, inner_owner, inner_row, *got_inner, got[0], got[1], got[2],
        flops=inner_flops + own_flops, unread=3,
    )
    losses, near_w, far_w, far_rows, *grads = call(
        functools.partial(main_kernel, outer),
        [
            shape((1, rows), f32),
            shape((rows + inner.total, rows), bf16),
            shape((outer.total, rows), bf16),
            shape((outer.total, width // outer.split), bf16),
            *outer_blocks,
        ],
        queries, scores, times, positives.reshape(1, rows), outer_owner, *got,
        flops=2 * far_flops,
    )
    back = exchange(outer, grads, -1)
    query_grads = call(
        functools.partial(query_grad_kernel, outer),
        shape((rows, width), bf16),
        near_w, documents, inner_rows, far_w, far_rows,
        flops=far_flops + inner_flops + own_flops,
    )
    grads_inner = call(
        functools.partial(inner_grad_kernel, inner),
        inner_blocks,
        near_w, queries,
        flops=inner_flops, unread=0,
    )
    back_inner = exchange(inner, grads_inner, -1)
    near_grads = call(
        functools.partial(near_grad_kernel, inner),
        shape((rows, width), f32),
        near_w, queries, inner_owner, inner_row, *back_inner, back[0], back[1], back[2],
        scratch=inner_codes, flops=inner_flops + own_flops, unread=3,
    )
    doc_grads = call(
        functools.partial(doc_grad_kernel, outer),
        shape((rows, width), bf16),
        near_grads, outer_owner, outer_row, *back,
        scratch=outer_codes, flops=far_flops,
    )
    return losses.reshape(rows), query_grads, doc_grads


def solution(mesh):
    return jax.shard_map(
        per_device,
        mesh=mesh,
        in_specs=(
            P(("grp", "dp"), None),
            P(("grp", "dp"), None),
            P(("grp", "dp")),
            P("grp", None, None),
            P("grp", None, None),
            P("dp", None, None, None),
            P("dp", None, None, None),
        ),
        out_specs=(P(("grp", "dp")), P(("grp", "dp"), None), P(("grp", "dp"), None)),
        check_vma=False,
    )
```

```python
import functools
from typing import NamedTuple

import jax
import jax.numpy as jnp
from jax import lax
from jax.experimental import pallas as pl
from jax.experimental.pallas import tpu as pltpu
from jax.sharding import PartitionSpec as P

COLUMNS = 4
ORDER = {("grp", 8): (4, 5, 3, 2, 7, 6, 1), ("dp", 4): (3, 2, 1)}
SCALE = 3.0
VMEM = pl.BlockSpec(memory_space=pltpu.VMEM)
ANY = pl.BlockSpec(memory_space=pl.ANY)
f32, bf16, i32 = jnp.float32, jnp.bfloat16, jnp.int32


def peer_at(axis, shift, sign, size, me=None):
    me = lax.axis_index(axis) if me is None else me
    return lax.rem(me + sign * shift + size, size) if axis == "grp" else lax.bitwise_xor(me, jnp.int32(shift))


class Blocks(NamedTuple):
    axis: str
    shifts: tuple
    count: int
    split: int

    @property
    def rows(self):
        return self.count * self.split

    @property
    def total(self):
        return self.rows * len(self.shifts)

    def part(self, n):
        return slice(n * self.rows, (n + 1) * self.rows)


def call(kernel, out_shape, *args, scratch=(), flops=0, unread=0, vmem=24):
    nbytes = sum(a.size * a.dtype.itemsize for a in (*args, *jax.tree.leaves(out_shape)))
    read = len(args) - unread

    def body(*refs):
        kernel(*refs[:read], *refs[len(args) :])

    return pl.pallas_call(
        body,
        out_shape=out_shape,
        in_specs=[VMEM] * read + [ANY] * unread,
        out_specs=jax.tree.map(lambda _: VMEM, out_shape),
        scratch_shapes=list(scratch),
        compiler_params=pltpu.CompilerParams(vmem_limit_bytes=vmem * 2**20),
        cost_estimate=pl.CostEstimate(flops=flops, bytes_accessed=nbytes, transcendentals=0),
    )(*args)


def dot(a, b, dims=((1,), (0,))):
    return lax.dot_general(a, b, (dims, ((), ())), preferred_element_type=f32)


NT = ((1,), (1,))
TN = ((0,), (0,))


def row_plan(plan):
    t = lax.broadcasted_iota(i32, (plan.rows, 128), 0)
    chunk = jnp.zeros_like(t)
    for c in range(1, plan.split):
        chunk = chunk + (t >= c * plan.count).astype(i32)
    slot = t - plan.count * chunk
    return jnp.concatenate([slot] * len(plan.shifts), axis=0), jnp.concatenate([chunk] * len(plan.shifts), axis=0)


def stacked(ref, split):
    width = ref.shape[1] // split
    return jnp.concatenate([ref[:, c * width : (c + 1) * width] for c in range(split)], axis=0)


def spread(values, chunk, split):
    if split == 1:
        return values.astype(bf16)
    return jnp.concatenate([jnp.where(chunk == c, values, 0.0).astype(bf16) for c in range(split)], axis=1)


def slot_codes(axis, owner_ref, codes):
    peers, rows = owner_ref.shape
    name = me = lax.axis_index(axis)
    if axis == "grp":
        name = lax.rem(me - lax.broadcasted_iota(i32, (peers, rows), 0) - 1 + 2 * peers, peers)
    wanted = owner_ref[...] == name
    earlier = lax.broadcasted_iota(i32, (rows, rows), 0) < lax.broadcasted_iota(i32, (rows, rows), 1)
    rank = dot(wanted.astype(f32).astype(bf16), earlier.astype(f32).astype(bf16))
    codes[...] = jnp.where(wanted, rank, -1.0).astype(i32)


def slot_onehot(plan, codes, row_ref):
    slot, chunk = row_plan(plan)
    asked = []
    for n, shift in enumerate(plan.shifts):
        r = peer_at(plan.axis, shift, 1, codes.shape[0])
        chosen = codes[pl.ds(r, 1), :] == slot[plan.part(n)]
        asked.append(jnp.where(chosen, row_ref[pl.ds(r, 1), :] + 1, 0).astype(f32))
    at = jnp.sum(jnp.concatenate(asked, axis=0), axis=1, keepdims=True)
    ids = lax.broadcasted_iota(i32, slot.shape, 1) + 1
    return jnp.where(ids.astype(f32) == at, 1.0, 0.0), chunk


def live_slots(plan, owner_ref):
    slot, _ = row_plan(plan)
    peers = owner_ref.shape[0]
    me = lax.axis_index(plan.axis)
    live = []
    for n, shift in enumerate(plan.shifts):
        name = peers - 1 - shift if plan.axis == "grp" else peer_at("dp", shift, -1, peers)
        used = jnp.sum((owner_ref[pl.ds(me, 1), :] == name).astype(f32), axis=1, keepdims=True)
        live.append(slot[plan.part(n)].astype(f32) < used)
    return jnp.concatenate(live, axis=0)


def send_kernel(plan, owner_ref, row_ref, docs_ref, *refs):
    *outs, codes = refs
    slot_codes(plan.axis, owner_ref, codes)
    onehot, chunk = slot_onehot(plan, codes, row_ref)
    rows = dot(spread(onehot, chunk, plan.split), stacked(docs_ref, plan.split))
    for n, out in enumerate(outs):
        out[...] = rows[plan.part(n)].astype(bf16)


def near_kernel(plan, q_ref, docs_ref, owner_ref, row_ref, *refs):
    *blocks, scores_out, times_out, inner_out = refs
    me = lax.axis_index("dp")
    rows = q_ref.shape[0]
    named = (owner_ref[pl.ds(me, 1), :] == me) & (row_ref[pl.ds(me, 1), :] == lax.broadcasted_iota(i32, (rows, rows), 0))
    times = 1.0 + jnp.sum(named.astype(f32), axis=1, keepdims=True)
    times_out[:rows, :] = jnp.broadcast_to(times, (rows, rows))
    times_out[rows:, :] = jnp.ones((plan.total, rows), f32)
    scores_out[:rows, :] = SCALE * dot(docs_ref[...], q_ref[...], NT)
    inner_out[...] = jnp.concatenate([block[...] for block in blocks], axis=0)
    scores = SCALE * dot(inner_out[...], q_ref[...], NT)
    scores_out[rows:, :] = jnp.where(live_slots(plan, owner_ref), scores, -jnp.inf)


def main_kernel(plan, q_ref, near_ref, times_ref, pos_ref, owner_ref, *refs):
    blocks, refs = refs[: len(plan.shifts)], refs[len(plan.shifts) :]
    loss_out, near_w, far_w, far, *grads = refs
    rows = q_ref.shape[0]
    _, chunk = row_plan(plan)
    far[...] = jnp.concatenate([block[...] for block in blocks], axis=0)
    width = far.shape[1]
    part = dot(far[...], q_ref[:, :width], NT)
    for c in range(1, plan.split):
        part = jnp.where(chunk == c, dot(far[...], q_ref[:, c * width : (c + 1) * width], NT), part)
    scores = []
    for n in range(len(blocks)):
        total = part[plan.part(n)]
        for c in range(1, plan.split):
            total = total + pltpu.roll(part[plan.part(n)], c * plan.count, 0)
        scores.append(total)
    scores = jnp.where(live_slots(plan, owner_ref), SCALE * jnp.concatenate(scores, axis=0), -jnp.inf)
    near = near_ref[...]
    top = jnp.maximum(jnp.max(near, axis=0, keepdims=True), jnp.max(scores, axis=0, keepdims=True))
    near_e = times_ref[...] * jnp.exp(near - top)
    far_e = jnp.exp(scores - top)
    total = jnp.sum(near_e, axis=0, keepdims=True)
    total = total + jnp.sum(jnp.where(chunk == 0, far_e, 0.0), axis=0, keepdims=True)
    factor = SCALE / total
    w = far_e * factor
    far_w[...] = w.astype(bf16)
    sums = dot(spread(w, chunk, plan.split), stacked(q_ref, plan.split))
    for n, out in enumerate(grads):
        out[...] = sums[plan.part(n)].astype(bf16)
    positive = (lax.broadcasted_iota(i32, near.shape, 0) == pos_ref[...]).astype(f32)
    loss_out[...] = top + jnp.log(total) - jnp.sum(jnp.where(positive > 0.0, near, 0.0), axis=0, keepdims=True)
    near_w[...] = (near_e * factor - SCALE * positive).astype(bf16)


def inner_grad_kernel(plan, near_w, q_ref, *outs):
    sums = dot(near_w[q_ref.shape[0] :, :], q_ref[...])
    for n, out in enumerate(outs):
        out[...] = sums[plan.part(n)].astype(bf16)


def add_far(plan, select, block, acc, cols):
    width = block.shape[1]
    chunk = cols.start // width
    if plan.split > 1:
        select = jnp.where(row_plan(plan)[1] == chunk, select, 0.0)
    return acc + dot(select.astype(bf16), block[:, cols.start - chunk * width : cols.stop - chunk * width], TN)


def query_grad_kernel(plan, near_w, docs_ref, inner_ref, far_w, far_ref, out):
    rows = docs_ref.shape[0]
    width = out.shape[1] // COLUMNS
    far_w = far_w[...].astype(f32)
    for c in range(COLUMNS):
        cols = slice(c * width, (c + 1) * width)
        acc = dot(near_w[:rows, :], docs_ref[:, cols], TN) + dot(near_w[rows:, :], inner_ref[:, cols], TN)
        out[:, cols] = add_far(plan, far_w, far_ref, acc, cols).astype(bf16)


def near_grad_kernel(plan, outer, near_w, q_ref, owner_ref, row_ref, outer_owner_ref, outer_row_ref, *refs):
    blocks, (out, *selects, codes, outer_codes) = refs[: len(plan.shifts)], refs[len(plan.shifts) :]
    slot_codes(outer.axis, outer_owner_ref, outer_codes)
    select, chunk = slot_onehot(outer, outer_codes, outer_row_ref)
    for c, select_out in enumerate(selects):
        select_out[...] = jnp.where(chunk == c, select, 0.0).astype(bf16)
    slot_codes(plan.axis, owner_ref, codes)
    onehot, _ = slot_onehot(plan, codes, row_ref)
    block = jnp.concatenate([block[...] for block in blocks], axis=0)
    out[...] = dot(near_w[: q_ref.shape[0], :], q_ref[...]) + dot(onehot.astype(bf16), block, TN)


def doc_grad_kernel(near_ref, *refs):
    *refs, out = refs
    split = out.shape[1] // refs[-1].shape[1]
    selects, blocks = refs[:split], refs[split:]
    block = jnp.concatenate([block[...] for block in blocks], axis=0)
    width = block.shape[1]
    for c, select in enumerate(selects):
        for half in range(2):
            cols = slice(half * width // 2, (half + 1) * width // 2)
            at = slice(c * width + cols.start, c * width + cols.stop)
            out[:, at] = (near_ref[:, at] + dot(select[...], block[:, cols], TN)).astype(bf16)


def exchange(plan, blocks, back=False):
    size = lax.axis_size(plan.axis)
    moved = []
    for shift, block in zip(plan.shifts, blocks):
        there = [(g, (g + shift) % size if plan.axis == "grp" else g ^ shift) for g in range(size)]
        moved.append(lax.ppermute(block, plan.axis, [(b, a) for a, b in there] if back else there))
    return moved


def per_device(queries, documents, positives, inner_owner, inner_row, outer_owner, outer_row):
    rows, width = queries.shape
    dp, grp = lax.axis_size("dp"), lax.axis_size("grp")
    cap_inner = -(-max(2, 2 * rows // dp) // 16) * 16
    cap_outer = -(-max(2, 2 * rows // (grp - 1)) // 4) * 4
    inner = Blocks("dp", ORDER.get(("dp", dp), tuple(range(1, dp))), cap_inner, 1)
    outer_shifts = ORDER.get(("grp", grp), tuple(range(1, grp)))
    outer = Blocks("grp", outer_shifts, cap_outer, 1 if cap_outer % 8 == 0 else 2)
    inner_owner, inner_row = inner_owner.reshape(dp, rows), inner_row.reshape(dp, rows)
    outer_owner, outer_row = outer_owner.reshape(grp, rows), outer_row.reshape(grp, rows)
    shape = jax.ShapeDtypeStruct
    outer_blocks = [shape((outer.rows, width // outer.split), bf16)] * len(outer.shifts)
    inner_blocks = [shape((inner.rows, width), bf16)] * len(inner.shifts)
    outer_codes, inner_codes = [pltpu.VMEM((grp, rows), i32)], [pltpu.VMEM((dp, rows), i32)]
    far_flops, inner_flops, own_flops = 2 * outer.total * rows * width, 2 * inner.total * rows * width, 2 * rows * rows * width

    send = call(
        functools.partial(send_kernel, outer._replace(shifts=outer.shifts[:1])),
        outer_blocks[:1],
        outer_owner, outer_row, documents,
        scratch=outer_codes, flops=far_flops,
    )
    send += call(
        functools.partial(send_kernel, outer._replace(shifts=outer.shifts[1:])),
        outer_blocks[1:],
        outer_owner, outer_row, documents, send[0],
        scratch=outer_codes, flops=far_flops, unread=1,
    )
    got = exchange(outer, send)
    send_inner = call(
        functools.partial(send_kernel, inner),
        inner_blocks,
        inner_owner, inner_row, documents,
        scratch=inner_codes, flops=inner_flops,
    )
    got_inner = exchange(inner, send_inner)
    scores, times, inner_rows = call(
        functools.partial(near_kernel, inner),
        [shape((rows + inner.total, rows), f32)] * 2 + [shape((inner.total, width), bf16)],
        queries, documents, inner_owner, inner_row, *got_inner, got[0], got[1], got[2],
        flops=inner_flops + own_flops, unread=3,
    )
    losses, near_w, far_w, far_rows, *grads = call(
        functools.partial(main_kernel, outer),
        [
            shape((1, rows), f32),
            shape((rows + inner.total, rows), bf16),
            shape((outer.total, rows), bf16),
            shape((outer.total, width // outer.split), bf16),
            *outer_blocks,
        ],
        queries, scores, times, positives.reshape(1, rows), outer_owner, *got,
        flops=2 * far_flops,
    )
    back = exchange(outer, grads, back=True)
    query_grads = call(
        functools.partial(query_grad_kernel, outer),
        shape((rows, width), bf16),
        near_w, documents, inner_rows, far_w, far_rows,
        flops=far_flops + inner_flops + own_flops,
    )
    grads_inner = call(
        functools.partial(inner_grad_kernel, inner),
        inner_blocks,
        near_w, queries,
        flops=inner_flops,
    )
    back_inner = exchange(inner, grads_inner, back=True)
    near_grads, *selects = call(
        functools.partial(near_grad_kernel, inner, outer),
        [shape((rows, width), f32)] + [shape((outer.total, rows), bf16)] * outer.split,
        near_w, queries, inner_owner, inner_row, outer_owner, outer_row, *back_inner, back[0], back[1], back[2],
        scratch=inner_codes + outer_codes, flops=inner_flops + own_flops, unread=3,
    )
    doc_grads = call(doc_grad_kernel, shape((rows, width), bf16), near_grads, *selects, *back, flops=far_flops)
    return losses.reshape(rows), query_grads, doc_grads


def solution(mesh):
    return jax.shard_map(
        per_device,
        mesh=mesh,
        in_specs=(
            P(("grp", "dp"), None),
            P(("grp", "dp"), None),
            P(("grp", "dp")),
            P("grp", None, None),
            P("grp", None, None),
            P("dp", None, None, None),
            P("dp", None, None, None),
        ),
        out_specs=(P(("grp", "dp")), P(("grp", "dp"), None), P(("grp", "dp"), None)),
        check_vma=False,
    )
```

```python
import functools
from typing import NamedTuple

import jax
import jax.numpy as jnp
from jax import lax
from jax.experimental import pallas as pl
from jax.experimental.pallas import tpu as pltpu
from jax.sharding import PartitionSpec as P

COLUMNS = 4
ORDER = {("grp", 8): (4, 5, 3, 2, 7, 6, 1), ("dp", 4): (3, 2, 1)}
SCALE = 3.0
VMEM = pl.BlockSpec(memory_space=pltpu.VMEM)
ANY = pl.BlockSpec(memory_space=pl.ANY)
f32, bf16, i32 = jnp.float32, jnp.bfloat16, jnp.int32


def peer_at(axis, shift, sign, size, me=None):
    me = lax.axis_index(axis) if me is None else me
    return lax.rem(me + sign * shift + size, size) if axis == "grp" else lax.bitwise_xor(me, jnp.int32(shift))


class Blocks(NamedTuple):
    axis: str
    shifts: tuple
    count: int
    split: int

    @property
    def rows(self):
        return self.count * self.split

    @property
    def total(self):
        return self.rows * len(self.shifts)

    def part(self, n):
        return slice(n * self.rows, (n + 1) * self.rows)


def call(kernel, out_shape, *args, scratch=(), flops=0, unread=0, vmem=12):
    nbytes = sum(a.size * a.dtype.itemsize for a in (*args, *jax.tree.leaves(out_shape)))
    read = len(args) - unread

    def body(*refs):
        kernel(*refs[:read], *refs[len(args) :])

    return pl.pallas_call(
        body,
        out_shape=out_shape,
        in_specs=[VMEM] * read + [ANY] * unread,
        out_specs=jax.tree.map(lambda _: VMEM, out_shape),
        scratch_shapes=list(scratch),
        compiler_params=pltpu.CompilerParams(vmem_limit_bytes=vmem * 2**20),
        cost_estimate=pl.CostEstimate(flops=flops, bytes_accessed=nbytes, transcendentals=0),
    )(*args)


def dot(a, b, dims=((1,), (0,))):
    return lax.dot_general(a, b, (dims, ((), ())), preferred_element_type=f32)


NT = ((1,), (1,))
TN = ((0,), (0,))


def row_plan(plan):
    t = lax.broadcasted_iota(i32, (plan.rows, 128), 0)
    chunk = jnp.zeros_like(t)
    for c in range(1, plan.split):
        chunk = chunk + (t >= c * plan.count).astype(i32)
    slot = t - plan.count * chunk
    return jnp.concatenate([slot] * len(plan.shifts), axis=0), jnp.concatenate([chunk] * len(plan.shifts), axis=0)


def stacked(ref, split):
    width = ref.shape[1] // split
    return jnp.concatenate([ref[:, c * width : (c + 1) * width] for c in range(split)], axis=0)


def spread(values, chunk, split):
    if split == 1:
        return values.astype(bf16)
    return jnp.concatenate([jnp.where(chunk == c, values, 0.0).astype(bf16) for c in range(split)], axis=1)


def slot_codes(axis, owner_ref, codes):
    peers, rows = owner_ref.shape
    name = me = lax.axis_index(axis)
    if axis == "grp":
        name = lax.rem(me - lax.broadcasted_iota(i32, (peers, rows), 0) - 1 + 2 * peers, peers)
    wanted = owner_ref[...] == name
    earlier = lax.broadcasted_iota(i32, (rows, rows), 0) < lax.broadcasted_iota(i32, (rows, rows), 1)
    rank = dot(wanted.astype(f32).astype(bf16), earlier.astype(f32).astype(bf16))
    codes[...] = jnp.where(wanted, rank, -1.0).astype(i32)


def slot_onehot(plan, codes, row_ref):
    slot, chunk = row_plan(plan)
    asked = []
    for n, shift in enumerate(plan.shifts):
        r = peer_at(plan.axis, shift, 1, codes.shape[0])
        chosen = codes[pl.ds(r, 1), :] == slot[plan.part(n)]
        asked.append(jnp.where(chosen, row_ref[pl.ds(r, 1), :] + 1, 0).astype(f32))
    at = jnp.sum(jnp.concatenate(asked, axis=0), axis=1, keepdims=True)
    ids = lax.broadcasted_iota(i32, slot.shape, 1) + 1
    return jnp.where(ids.astype(f32) == at, 1.0, 0.0), chunk


def live_slots(plan, owner_ref):
    slot, _ = row_plan(plan)
    peers = owner_ref.shape[0]
    me = lax.axis_index(plan.axis)
    live = []
    for n, shift in enumerate(plan.shifts):
        name = peers - 1 - shift if plan.axis == "grp" else peer_at("dp", shift, -1, peers)
        used = jnp.sum((owner_ref[pl.ds(me, 1), :] == name).astype(f32), axis=1, keepdims=True)
        live.append(slot[plan.part(n)].astype(f32) < used)
    return jnp.concatenate(live, axis=0)


def send_kernel(plan, owner_ref, row_ref, docs_ref, *refs):
    *outs, codes = refs
    slot_codes(plan.axis, owner_ref, codes)
    onehot, chunk = slot_onehot(plan, codes, row_ref)
    rows = dot(spread(onehot, chunk, plan.split), stacked(docs_ref, plan.split))
    for n, out in enumerate(outs):
        out[...] = rows[plan.part(n)].astype(bf16)


def near_kernel(plan, q_ref, docs_ref, owner_ref, row_ref, *refs):
    *blocks, scores_out, times_out, inner_out = refs
    me = lax.axis_index("dp")
    rows = q_ref.shape[0]
    named = (owner_ref[pl.ds(me, 1), :] == me) & (row_ref[pl.ds(me, 1), :] == lax.broadcasted_iota(i32, (rows, rows), 0))
    times = 1.0 + jnp.sum(named.astype(f32), axis=1, keepdims=True)
    times_out[:rows, :] = jnp.broadcast_to(times, (rows, rows))
    times_out[rows:, :] = jnp.ones((plan.total, rows), f32)
    scores_out[:rows, :] = SCALE * dot(docs_ref[...], q_ref[...], NT)
    inner_out[...] = jnp.concatenate([block[...] for block in blocks], axis=0)
    scores = SCALE * dot(inner_out[...], q_ref[...], NT)
    scores_out[rows:, :] = jnp.where(live_slots(plan, owner_ref), scores, -jnp.inf)


def main_kernel(plan, q_ref, near_ref, times_ref, pos_ref, owner_ref, *refs):
    blocks, refs = refs[: len(plan.shifts)], refs[len(plan.shifts) :]
    loss_out, near_w, far_w, far, *grads = refs
    rows = q_ref.shape[0]
    _, chunk = row_plan(plan)
    far[...] = jnp.concatenate([block[...] for block in blocks], axis=0)
    width = far.shape[1]
    part = dot(far[...], q_ref[:, :width], NT)
    for c in range(1, plan.split):
        part = jnp.where(chunk == c, dot(far[...], q_ref[:, c * width : (c + 1) * width], NT), part)
    scores = []
    for n in range(len(blocks)):
        total = part[plan.part(n)]
        for c in range(1, plan.split):
            total = total + pltpu.roll(part[plan.part(n)], c * plan.count, 0)
        scores.append(total)
    scores = jnp.where(live_slots(plan, owner_ref), SCALE * jnp.concatenate(scores, axis=0), -jnp.inf)
    near = near_ref[...]
    top = jnp.maximum(jnp.max(near, axis=0, keepdims=True), jnp.max(scores, axis=0, keepdims=True))
    near_e = times_ref[...] * jnp.exp(near - top)
    far_e = jnp.exp(scores - top)
    total = jnp.sum(near_e, axis=0, keepdims=True)
    total = total + jnp.sum(jnp.where(chunk == 0, far_e, 0.0), axis=0, keepdims=True)
    factor = SCALE / total
    w = far_e * factor
    far_w[...] = w.astype(bf16)
    sums = dot(spread(w, chunk, plan.split), stacked(q_ref, plan.split))
    for n, out in enumerate(grads):
        out[...] = sums[plan.part(n)].astype(bf16)
    positive = (lax.broadcasted_iota(i32, near.shape, 0) == pos_ref[...]).astype(f32)
    loss_out[...] = top + jnp.log(total) - jnp.sum(jnp.where(positive > 0.0, near, 0.0), axis=0, keepdims=True)
    near_w[...] = (near_e * factor - SCALE * positive).astype(bf16)


def inner_grad_kernel(plan, near_w, q_ref, *outs):
    sums = dot(near_w[q_ref.shape[0] :, :], q_ref[...])
    for n, out in enumerate(outs):
        out[...] = sums[plan.part(n)].astype(bf16)


def add_far(plan, select, block, acc, cols):
    width = block.shape[1]
    chunk = cols.start // width
    if plan.split > 1:
        select = jnp.where(row_plan(plan)[1] == chunk, select, 0.0)
    return acc + dot(select.astype(bf16), block[:, cols.start - chunk * width : cols.stop - chunk * width], TN)


def query_grad_kernel(plan, near_w, docs_ref, inner_ref, far_w, far_ref, out):
    rows = docs_ref.shape[0]
    width = out.shape[1] // COLUMNS
    far_w = far_w[...].astype(f32)
    for c in range(COLUMNS):
        cols = slice(c * width, (c + 1) * width)
        acc = dot(near_w[:rows, :], docs_ref[:, cols], TN) + dot(near_w[rows:, :], inner_ref[:, cols], TN)
        out[:, cols] = add_far(plan, far_w, far_ref, acc, cols).astype(bf16)


def near_grad_kernel(plan, outer, near_w, q_ref, owner_ref, row_ref, outer_owner_ref, outer_row_ref, *refs):
    blocks, (out, *selects, codes, outer_codes) = refs[: len(plan.shifts)], refs[len(plan.shifts) :]
    slot_codes(outer.axis, outer_owner_ref, outer_codes)
    select, chunk = slot_onehot(outer, outer_codes, outer_row_ref)
    for c, select_out in enumerate(selects):
        select_out[...] = jnp.where(chunk == c, select, 0.0).astype(bf16)
    slot_codes(plan.axis, owner_ref, codes)
    onehot, _ = slot_onehot(plan, codes, row_ref)
    block = jnp.concatenate([block[...] for block in blocks], axis=0)
    out[...] = dot(near_w[: q_ref.shape[0], :], q_ref[...]) + dot(onehot.astype(bf16), block, TN)


def doc_grad_kernel(near_ref, *refs):
    *refs, out = refs
    split = out.shape[1] // refs[-1].shape[1]
    selects, blocks = refs[:split], refs[split:]
    block = jnp.concatenate([block[...] for block in blocks], axis=0)
    width = block.shape[1]
    for c, select in enumerate(selects):
        for half in range(2):
            cols = slice(half * width // 2, (half + 1) * width // 2)
            at = slice(c * width + cols.start, c * width + cols.stop)
            out[:, at] = (near_ref[:, at] + dot(select[...], block[:, cols], TN)).astype(bf16)


def exchange(plan, blocks, back=False):
    size = lax.axis_size(plan.axis)
    moved = []
    for shift, block in zip(plan.shifts, blocks):
        there = [(g, (g + shift) % size if plan.axis == "grp" else g ^ shift) for g in range(size)]
        moved.append(lax.ppermute(block, plan.axis, [(b, a) for a, b in there] if back else there))
    return moved


def per_device(queries, documents, positives, inner_owner, inner_row, outer_owner, outer_row):
    rows, width = queries.shape
    dp, grp = lax.axis_size("dp"), lax.axis_size("grp")
    cap_inner = -(-max(2, 2 * rows // dp) // 16) * 16
    cap_outer = -(-max(2, 2 * rows // (grp - 1)) // 4) * 4
    inner = Blocks("dp", ORDER.get(("dp", dp), tuple(range(1, dp))), cap_inner, 1)
    outer_shifts = ORDER.get(("grp", grp), tuple(range(1, grp)))
    outer = Blocks("grp", outer_shifts, cap_outer, 1 if cap_outer % 8 == 0 else 2)
    inner_owner, inner_row = inner_owner.reshape(dp, rows), inner_row.reshape(dp, rows)
    outer_owner, outer_row = outer_owner.reshape(grp, rows), outer_row.reshape(grp, rows)
    shape = jax.ShapeDtypeStruct
    outer_blocks = [shape((outer.rows, width // outer.split), bf16)] * len(outer.shifts)
    inner_blocks = [shape((inner.rows, width), bf16)] * len(inner.shifts)
    outer_codes, inner_codes = [pltpu.VMEM((grp, rows), i32)], [pltpu.VMEM((dp, rows), i32)]
    far_flops, inner_flops, own_flops = 2 * outer.total * rows * width, 2 * inner.total * rows * width, 2 * rows * rows * width

    send = call(
        functools.partial(send_kernel, outer._replace(shifts=outer.shifts[:1])),
        outer_blocks[:1],
        outer_owner, outer_row, documents,
        scratch=outer_codes, flops=far_flops,
    )
    send += call(
        functools.partial(send_kernel, outer._replace(shifts=outer.shifts[1:])),
        outer_blocks[1:],
        outer_owner, outer_row, documents, send[0],
        scratch=outer_codes, flops=far_flops, unread=1,
    )
    got = exchange(outer, send)
    send_inner = call(
        functools.partial(send_kernel, inner),
        inner_blocks,
        inner_owner, inner_row, documents,
        scratch=inner_codes, flops=inner_flops,
    )
    got_inner = exchange(inner, send_inner)
    scores, times, inner_rows = call(
        functools.partial(near_kernel, inner),
        [shape((rows + inner.total, rows), f32)] * 2 + [shape((inner.total, width), bf16)],
        queries, documents, inner_owner, inner_row, *got_inner, got[0], got[1], got[2],
        flops=inner_flops + own_flops, unread=3,
    )
    losses, near_w, far_w, far_rows, *grads = call(
        functools.partial(main_kernel, outer),
        [
            shape((1, rows), f32),
            shape((rows + inner.total, rows), bf16),
            shape((outer.total, rows), bf16),
            shape((outer.total, width // outer.split), bf16),
            *outer_blocks,
        ],
        queries, scores, times, positives.reshape(1, rows), outer_owner, *got,
        flops=2 * far_flops,
    )
    back = exchange(outer, grads, back=True)
    query_grads = call(
        functools.partial(query_grad_kernel, outer),
        shape((rows, width), bf16),
        near_w, documents, inner_rows, far_w, far_rows,
        flops=far_flops + inner_flops + own_flops,
    )
    grads_inner = call(
        functools.partial(inner_grad_kernel, inner),
        inner_blocks,
        near_w, queries,
        flops=inner_flops,
    )
    back_inner = exchange(inner, grads_inner, back=True)
    near_grads, *selects = call(
        functools.partial(near_grad_kernel, inner, outer),
        [shape((rows, width), f32)] + [shape((outer.total, rows), bf16)] * outer.split,
        near_w, queries, inner_owner, inner_row, outer_owner, outer_row, *back_inner, back[0], back[1], back[2],
        scratch=inner_codes + outer_codes, flops=inner_flops + own_flops, unread=3,
    )
    doc_grads = call(doc_grad_kernel, shape((rows, width), bf16), near_grads, *selects, *back, flops=far_flops)
    return losses.reshape(rows), query_grads, doc_grads


def solution(mesh):
    return jax.shard_map(
        per_device,
        mesh=mesh,
        in_specs=(
            P(("grp", "dp"), None),
            P(("grp", "dp"), None),
            P(("grp", "dp")),
            P("grp", None, None),
            P("grp", None, None),
            P("dp", None, None, None),
            P("dp", None, None, None),
        ),
        out_specs=(P(("grp", "dp")), P(("grp", "dp"), None), P(("grp", "dp"), None)),
        check_vma=False,
    )
```

```python
import functools
from typing import NamedTuple

import jax
import jax.numpy as jnp
from jax import lax
from jax.experimental import pallas as pl
from jax.experimental.pallas import tpu as pltpu
from jax.sharding import PartitionSpec as P

COLUMNS = 4
ORDER = {("grp", 8): (4, 5, 3, 2, 7, 6, 1), ("dp", 4): (3, 2, 1)}
SCALE = 3.0
VMEM = pl.BlockSpec(memory_space=pltpu.VMEM)
ANY = pl.BlockSpec(memory_space=pl.ANY)
f32, bf16, i32 = jnp.float32, jnp.bfloat16, jnp.int32


def peer_at(axis, shift, sign, size, me=None):
    me = lax.axis_index(axis) if me is None else me
    return lax.rem(me + sign * shift + size, size) if axis == "grp" else lax.bitwise_xor(me, jnp.int32(shift))


class Blocks(NamedTuple):
    axis: str
    shifts: tuple
    count: int
    split: int

    @property
    def rows(self):
        return self.count * self.split

    @property
    def total(self):
        return self.rows * len(self.shifts)

    def part(self, n):
        return slice(n * self.rows, (n + 1) * self.rows)


def call(kernel, out_shape, *args, scratch=(), flops=0, unread=0, vmem=12):
    nbytes = sum(a.size * a.dtype.itemsize for a in (*args, *jax.tree.leaves(out_shape)))
    read = len(args) - unread

    def body(*refs):
        kernel(*refs[:read], *refs[len(args) :])

    return pl.pallas_call(
        body,
        out_shape=out_shape,
        in_specs=[VMEM] * read + [ANY] * unread,
        out_specs=jax.tree.map(lambda _: VMEM, out_shape),
        scratch_shapes=list(scratch),
        compiler_params=pltpu.CompilerParams(vmem_limit_bytes=vmem * 2**20),
        cost_estimate=pl.CostEstimate(flops=flops, bytes_accessed=nbytes, transcendentals=0),
    )(*args)


def dot(a, b, dims=((1,), (0,))):
    return lax.dot_general(a, b, (dims, ((), ())), preferred_element_type=f32)


NT = ((1,), (1,))
TN = ((0,), (0,))


def row_plan(plan):
    t = lax.broadcasted_iota(i32, (plan.rows, 128), 0)
    chunk = jnp.zeros_like(t)
    for c in range(1, plan.split):
        chunk = chunk + (t >= c * plan.count).astype(i32)
    slot = t - plan.count * chunk
    return jnp.concatenate([slot] * len(plan.shifts), axis=0), jnp.concatenate([chunk] * len(plan.shifts), axis=0)


def stacked(ref, split):
    width = ref.shape[1] // split
    return jnp.concatenate([ref[:, c * width : (c + 1) * width] for c in range(split)], axis=0)


def spread(values, chunk, split):
    if split == 1:
        return values.astype(bf16)
    return jnp.concatenate([jnp.where(chunk == c, values, 0.0).astype(bf16) for c in range(split)], axis=1)


def slot_codes(axis, owner_ref, codes):
    peers, rows = owner_ref.shape
    name = me = lax.axis_index(axis)
    if axis == "grp":
        name = lax.rem(me - lax.broadcasted_iota(i32, (peers, rows), 0) - 1 + 2 * peers, peers)
    wanted = owner_ref[...] == name
    earlier = lax.broadcasted_iota(i32, (rows, rows), 0) < lax.broadcasted_iota(i32, (rows, rows), 1)
    rank = dot(wanted.astype(f32).astype(bf16), earlier.astype(f32).astype(bf16))
    codes[...] = jnp.where(wanted, rank, -1.0).astype(i32)


def slot_onehot(plan, codes, row_ref):
    slot, chunk = row_plan(plan)
    asked = []
    for n, shift in enumerate(plan.shifts):
        r = peer_at(plan.axis, shift, 1, codes.shape[0])
        chosen = codes[pl.ds(r, 1), :] == slot[plan.part(n)]
        asked.append(jnp.where(chosen, row_ref[pl.ds(r, 1), :] + 1, 0).astype(f32))
    at = jnp.sum(jnp.concatenate(asked, axis=0), axis=1, keepdims=True)
    ids = lax.broadcasted_iota(i32, slot.shape, 1) + 1
    return jnp.where(ids.astype(f32) == at, 1.0, 0.0), chunk


def live_slots(plan, owner_ref):
    slot, _ = row_plan(plan)
    peers = owner_ref.shape[0]
    me = lax.axis_index(plan.axis)
    live = []
    for n, shift in enumerate(plan.shifts):
        name = peers - 1 - shift if plan.axis == "grp" else peer_at("dp", shift, -1, peers)
        used = jnp.sum((owner_ref[pl.ds(me, 1), :] == name).astype(f32), axis=1, keepdims=True)
        live.append(slot[plan.part(n)].astype(f32) < used)
    return jnp.concatenate(live, axis=0)


def send_kernel(plan, owner_ref, row_ref, docs_ref, *refs):
    *outs, codes = refs
    slot_codes(plan.axis, owner_ref, codes)
    onehot, chunk = slot_onehot(plan, codes, row_ref)
    rows = dot(spread(onehot, chunk, plan.split), stacked(docs_ref, plan.split))
    for n, out in enumerate(outs):
        out[...] = rows[plan.part(n)].astype(bf16)


def near_kernel(plan, q_ref, docs_ref, owner_ref, row_ref, *refs):
    *blocks, scores_out, times_out, inner_out = refs
    me = lax.axis_index("dp")
    rows = q_ref.shape[0]
    named = (owner_ref[pl.ds(me, 1), :] == me) & (row_ref[pl.ds(me, 1), :] == lax.broadcasted_iota(i32, (rows, rows), 0))
    times = 1.0 + jnp.sum(named.astype(f32), axis=1, keepdims=True)
    times_out[...] = jnp.broadcast_to(times, (rows, rows))
    scores_out[:rows, :] = SCALE * dot(docs_ref[...], q_ref[...], NT)
    inner_out[...] = jnp.concatenate([block[...] for block in blocks], axis=0)
    scores = SCALE * dot(inner_out[...], q_ref[...], NT)
    scores_out[rows:, :] = jnp.where(live_slots(plan, owner_ref), scores, -jnp.inf)


def main_kernel(plan, q_ref, near_ref, times_ref, pos_ref, owner_ref, *refs):
    blocks, refs = refs[: len(plan.shifts)], refs[len(plan.shifts) :]
    loss_out, near_w, far_w, far, *grads = refs
    rows = q_ref.shape[0]
    _, chunk = row_plan(plan)
    far[...] = jnp.concatenate([block[...] for block in blocks], axis=0)
    width = far.shape[1]
    part = dot(far[...], q_ref[:, :width], NT)
    for c in range(1, plan.split):
        part = jnp.where(chunk == c, dot(far[...], q_ref[:, c * width : (c + 1) * width], NT), part)
    scores = []
    for n in range(len(blocks)):
        total = part[plan.part(n)]
        for c in range(1, plan.split):
            total = total + pltpu.roll(part[plan.part(n)], c * plan.count, 0)
        scores.append(total)
    scores = jnp.where(live_slots(plan, owner_ref), SCALE * jnp.concatenate(scores, axis=0), -jnp.inf)
    near = near_ref[...]
    top = jnp.maximum(jnp.max(near, axis=0, keepdims=True), jnp.max(scores, axis=0, keepdims=True))
    near_e = jnp.exp(near - top)
    own = times_ref.shape[0]
    near_e = jnp.concatenate([times_ref[...] * near_e[:own], near_e[own:]], axis=0)
    far_e = jnp.exp(scores - top)
    total = jnp.sum(near_e, axis=0, keepdims=True)
    total = total + jnp.sum(jnp.where(chunk == 0, far_e, 0.0), axis=0, keepdims=True)
    factor = SCALE / total
    w = far_e * factor
    far_w[...] = w.astype(bf16)
    sums = dot(spread(w, chunk, plan.split), stacked(q_ref, plan.split))
    for n, out in enumerate(grads):
        out[...] = sums[plan.part(n)].astype(bf16)
    positive = (lax.broadcasted_iota(i32, near.shape, 0) == pos_ref[...]).astype(f32)
    loss_out[...] = top + jnp.log(total) - jnp.sum(jnp.where(positive > 0.0, near, 0.0), axis=0, keepdims=True)
    near_w[...] = (near_e * factor - SCALE * positive).astype(bf16)


def inner_grad_kernel(plan, near_w, q_ref, *outs):
    sums = dot(near_w[q_ref.shape[0] :, :], q_ref[...])
    for n, out in enumerate(outs):
        out[...] = sums[plan.part(n)].astype(bf16)


def add_far(plan, select, block, acc, cols):
    width = block.shape[1]
    chunk = cols.start // width
    if plan.split > 1:
        select = jnp.where(row_plan(plan)[1] == chunk, select, 0.0)
    return acc + dot(select.astype(bf16), block[:, cols.start - chunk * width : cols.stop - chunk * width], TN)


def query_grad_kernel(plan, near_w, docs_ref, inner_ref, far_w, far_ref, out):
    rows = docs_ref.shape[0]
    width = out.shape[1] // COLUMNS
    far_w = far_w[...].astype(f32)
    for c in range(COLUMNS):
        cols = slice(c * width, (c + 1) * width)
        acc = dot(near_w[:rows, :], docs_ref[:, cols], TN) + dot(near_w[rows:, :], inner_ref[:, cols], TN)
        out[:, cols] = add_far(plan, far_w, far_ref, acc, cols).astype(bf16)


def near_grad_kernel(plan, outer, near_w, q_ref, owner_ref, row_ref, outer_owner_ref, outer_row_ref, *refs):
    blocks, (out, *selects, codes, outer_codes) = refs[: len(plan.shifts)], refs[len(plan.shifts) :]
    slot_codes(outer.axis, outer_owner_ref, outer_codes)
    select, chunk = slot_onehot(outer, outer_codes, outer_row_ref)
    for c, select_out in enumerate(selects):
        select_out[...] = jnp.where(chunk == c, select, 0.0).astype(bf16)
    slot_codes(plan.axis, owner_ref, codes)
    onehot, _ = slot_onehot(plan, codes, row_ref)
    block = jnp.concatenate([block[...] for block in blocks], axis=0)
    out[...] = dot(near_w[: q_ref.shape[0], :], q_ref[...]) + dot(onehot.astype(bf16), block, TN)


def doc_grad_kernel(near_ref, *refs):
    *refs, out = refs
    split = out.shape[1] // refs[-1].shape[1]
    selects, blocks = refs[:split], refs[split:]
    block = jnp.concatenate([block[...] for block in blocks], axis=0)
    width = block.shape[1]
    for c, select in enumerate(selects):
        for half in range(2):
            cols = slice(half * width // 2, (half + 1) * width // 2)
            at = slice(c * width + cols.start, c * width + cols.stop)
            out[:, at] = (near_ref[:, at] + dot(select[...], block[:, cols], TN)).astype(bf16)


def exchange(plan, blocks, back=False):
    size = lax.axis_size(plan.axis)
    moved = []
    for shift, block in zip(plan.shifts, blocks):
        there = [(g, (g + shift) % size if plan.axis == "grp" else g ^ shift) for g in range(size)]
        moved.append(lax.ppermute(block, plan.axis, [(b, a) for a, b in there] if back else there))
    return moved


def per_device(queries, documents, positives, inner_owner, inner_row, outer_owner, outer_row):
    rows, width = queries.shape
    dp, grp = lax.axis_size("dp"), lax.axis_size("grp")
    cap_inner = -(-max(2, 2 * rows // dp) // 16) * 16
    cap_outer = -(-max(2, 2 * rows // (grp - 1)) // 4) * 4
    inner = Blocks("dp", ORDER.get(("dp", dp), tuple(range(1, dp))), cap_inner, 1)
    outer_shifts = ORDER.get(("grp", grp), tuple(range(1, grp)))
    outer = Blocks("grp", outer_shifts, cap_outer, 1 if cap_outer % 8 == 0 else 2)
    inner_owner, inner_row = inner_owner.reshape(dp, rows), inner_row.reshape(dp, rows)
    outer_owner, outer_row = outer_owner.reshape(grp, rows), outer_row.reshape(grp, rows)
    shape = jax.ShapeDtypeStruct
    outer_blocks = [shape((outer.rows, width // outer.split), bf16)] * len(outer.shifts)
    inner_blocks = [shape((inner.rows, width), bf16)] * len(inner.shifts)
    outer_codes, inner_codes = [pltpu.VMEM((grp, rows), i32)], [pltpu.VMEM((dp, rows), i32)]
    far_flops, inner_flops, own_flops = 2 * outer.total * rows * width, 2 * inner.total * rows * width, 2 * rows * rows * width

    send = call(
        functools.partial(send_kernel, outer._replace(shifts=outer.shifts[:1])),
        outer_blocks[:1],
        outer_owner, outer_row, documents,
        scratch=outer_codes, flops=far_flops,
    )
    send += call(
        functools.partial(send_kernel, outer._replace(shifts=outer.shifts[1:])),
        outer_blocks[1:],
        outer_owner, outer_row, documents, send[0],
        scratch=outer_codes, flops=far_flops, unread=1,
    )
    got = exchange(outer, send)
    send_inner = call(
        functools.partial(send_kernel, inner),
        inner_blocks,
        inner_owner, inner_row, documents,
        scratch=inner_codes, flops=inner_flops,
    )
    got_inner = exchange(inner, send_inner)
    scores, times, inner_rows = call(
        functools.partial(near_kernel, inner),
        [shape((rows + inner.total, rows), f32), shape((rows, rows), f32)] + [shape((inner.total, width), bf16)],
        queries, documents, inner_owner, inner_row, *got_inner, got[0], got[1], got[2],
        flops=inner_flops + own_flops, unread=3,
    )
    losses, near_w, far_w, far_rows, *grads = call(
        functools.partial(main_kernel, outer),
        [
            shape((1, rows), f32),
            shape((rows + inner.total, rows), bf16),
            shape((outer.total, rows), bf16),
            shape((outer.total, width // outer.split), bf16),
            *outer_blocks,
        ],
        queries, scores, times, positives.reshape(1, rows), outer_owner, *got,
        flops=2 * far_flops,
    )
    back = exchange(outer, grads, back=True)
    query_grads = call(
        functools.partial(query_grad_kernel, outer),
        shape((rows, width), bf16),
        near_w, documents, inner_rows, far_w, far_rows,
        flops=far_flops + inner_flops + own_flops,
    )
    grads_inner = call(
        functools.partial(inner_grad_kernel, inner),
        inner_blocks,
        near_w, queries,
        flops=inner_flops,
    )
    back_inner = exchange(inner, grads_inner, back=True)
    near_grads, *selects = call(
        functools.partial(near_grad_kernel, inner, outer),
        [shape((rows, width), f32)] + [shape((outer.total, rows), bf16)] * outer.split,
        near_w, queries, inner_owner, inner_row, outer_owner, outer_row, *back_inner, back[0], back[1], back[2],
        scratch=inner_codes + outer_codes, flops=inner_flops + own_flops, unread=3,
    )
    doc_grads = call(doc_grad_kernel, shape((rows, width), bf16), near_grads, *selects, *back, flops=far_flops)
    return losses.reshape(rows), query_grads, doc_grads


def solution(mesh):
    return jax.shard_map(
        per_device,
        mesh=mesh,
        in_specs=(
            P(("grp", "dp"), None),
            P(("grp", "dp"), None),
            P(("grp", "dp")),
            P("grp", None, None),
            P("grp", None, None),
            P("dp", None, None, None),
            P("dp", None, None, None),
        ),
        out_specs=(P(("grp", "dp")), P(("grp", "dp"), None), P(("grp", "dp"), None)),
        check_vma=False,
    )
```
